128 devices in a mesh: ctx: 32 (over y_lo, z, x), fsdp: 4 (over y_hi, core).
Axes of the slice: x: 4, y: 4 (y_hi: 2, y_lo: 2; y = y_hi * 2 + y_lo), z: 4, core: 2. Of those that a mesh axis runs over, the one named last changes fastest.
Arguments:
- tokens: bfloat16 [4, 2, 4096, 640], P('fsdp', None, 'ctx'), may hold values from -6 to 6
- cotangent: bfloat16 [4, 2, 4096, 640], P('fsdp', None, 'ctx'), may hold values from -6 to 6
- lengths: int32 [4, 2], P('fsdp'), may hold values from 1024 to 4096, as said below
- block_order: int32 [64], replicated, may hold values from 0 to 63, each once
- query_weight: bfloat16 [640, 1024], P(None, 'fsdp'), may hold values from -0.25 to 0.25
- key_weight: bfloat16 [640, 256], P(None, 'fsdp'), may hold values from -0.25 to 0.25
- value_weight: bfloat16 [640, 256], P(None, 'fsdp'), may hold values from -0.25 to 0.25
- out_weight: bfloat16 [1024, 640], P('fsdp'), may hold values from -0.1875 to 0.1875
- gate_weight: bfloat16 [640, 2048], P(None, 'fsdp'), may hold values from -0.25 to 0.25
- up_weight: bfloat16 [640, 2048], P(None, 'fsdp'), may hold values from -0.25 to 0.25
- down_weight: bfloat16 [2048, 640], P('fsdp'), may hold values from -0.125 to 0.125
- gain_attn_in: bfloat16 [640], P('fsdp'), may hold values from -0.5 to 0.5
- gain_attn_out: bfloat16 [640], P('fsdp'), may hold values from -0.5 to 0.5
- gain_ffn_in: bfloat16 [640], P('fsdp'), may hold values from -0.5 to 0.5
- gain_ffn_out: bfloat16 [640], P('fsdp'), may hold values from -0.5 to 0.5
Outputs:
- result: bfloat16 [4, 2, 4096, 640], P('fsdp', None, 'ctx')
- token_grad: float32 [4, 2, 4096, 640], P('fsdp', None, 'ctx')
- query_grad: float32 [640, 1024], P(None, 'fsdp')
- key_grad: float32 [640, 256], P(None, 'fsdp')
- value_grad: float32 [640, 256], P(None, 'fsdp')
- out_grad: float32 [1024, 640], P('fsdp')
- gate_grad: float32 [640, 2048], P(None, 'fsdp')
- up_grad: float32 [640, 2048], P(None, 'fsdp')
- down_grad: float32 [2048, 640], P('fsdp')
- attn_in_grad: float32 [640], P('fsdp')
- attn_out_grad: float32 [640], P('fsdp')
- ffn_in_grad: float32 [640], P('fsdp')
- ffn_out_grad: float32 [640], P('fsdp')
The draws below stay inside these ranges and needn't reach their ends.
Inputs may be any that keep to these rules, and one draw needn't show every extreme that they name: `lengths`: in each group the sequence of one micro-batch, drawn from the seed, has exactly 4096 valid tokens; in one group, drawn from the seed, another sequence has exactly 1024.
All inputs are finite; a program needn't handle non-finite values.
Results may differ from the reference program's by a relative error of at most 0.03.
Values may be sent and summed in bfloat16 or wider, within the bound.
No kernel may reach another device: no remote copies, remote signals or barrier semaphores. Data moves between devices by JAX's collectives and lax.ppermute only.
A program may use at most 192 MiB of HBM per device.

```python
import jax
import jax.numpy as jnp
from jax import lax

D = 640
FF = 2048
H = 4
HD = 256
MB = 2
BLK = 64
SLOTS = 4096
NBLK = 64
GROUPS = 4


def draw_lengths(key, part):
    key = jax.random.fold_in(key, 7)
    pick_key, other_key, group_key = jax.random.split(key, 3)
    chosen = jax.random.randint(pick_key, (GROUPS,), 0, MB)
    others = jax.random.randint(other_key, (GROUPS, MB), SLOTS // 4, SLOTS + 1)
    short_group = jax.random.randint(group_key, (), 0, GROUPS)
    micro_slots = jnp.arange(MB, dtype=jnp.int32)
    group_slots = jnp.arange(GROUPS, dtype=jnp.int32)
    short_micro = (chosen + 1) % MB
    is_short = (group_slots[:, None] == short_group) & (micro_slots[None, :] == short_micro[:, None])
    others = jnp.where(is_short, SLOTS // 4, others)
    return jnp.where(micro_slots[None, :] == chosen[:, None], SLOTS, others).astype(jnp.int32)


def block_levels(key, dims, shards, least, largest):
    loudness, own = 1.0, jax.random.fold_in(key, 6)
    for dim, parts in shards:
        heights = jnp.exp(jax.random.uniform(jax.random.fold_in(own, dim), (parts,), jnp.float32, least / len(shards), largest / len(shards)))
        loudness = loudness * jnp.repeat(heights, dims[dim] // parts).reshape([-1 if axis == dim else 1 for axis in range(len(dims))])
    return loudness


def scatter_about(stream_key, extent, spread, reach, cuts=(), kind=jnp.bfloat16):
    factor_of = block_levels(stream_key, extent, cuts, -0.22, 0.18) if cuts else 1.0
    values = jax.random.normal(stream_key, extent, jnp.float32) * spread * factor_of
    return jnp.minimum(jnp.maximum(values, -reach), reach).astype(kind)


def setup_inputs(seed: int = 0) -> dict:
    key_list = jax.random.split(jax.random.key(seed), 16)
    tokens = scatter_about(key_list[0], (GROUPS, MB, SLOTS, D), 1.0, 6.0, ((0, 4), (2, 32)))
    cotangent = scatter_about(key_list[1], (GROUPS, MB, SLOTS, D), 1.0, 6.0, ((0, 4), (2, 32)))
    lengths = draw_lengths(jax.random.fold_in(key_list[15], 71), 0)
    block_order = jax.random.permutation(key_list[3], NBLK).astype(jnp.int32)
    query_weight = scatter_about(key_list[4], (D, H * HD), D ** -0.5, 0.25, ((1, 4),))
    key_weight = scatter_about(key_list[5], (D, HD), D ** -0.5, 0.25, ((1, 4),))
    value_weight = scatter_about(key_list[6], (D, HD), D ** -0.5, 0.25, ((1, 4),))
    out_weight = scatter_about(key_list[7], (H * HD, D), (H * HD) ** -0.5, 0.1875, ((0, 4),))
    gate_weight = scatter_about(key_list[8], (D, FF), D ** -0.5, 0.25, ((1, 4),))
    up_weight = scatter_about(key_list[9], (D, FF), D ** -0.5, 0.25, ((1, 4),))
    down_weight = scatter_about(key_list[10], (FF, D), FF ** -0.5, 0.125, ((0, 4),))
    gain_attn_in = jnp.clip(jax.random.uniform(key_list[11], (D,), jnp.float32, -0.5, 0.5) * block_levels(key_list[11], (D,), ((0, 4),), -0.4, 0.0), -0.5, 0.5).astype(jnp.bfloat16)
    gain_attn_out = jnp.clip(jax.random.uniform(key_list[12], (D,), jnp.float32, -0.5, 0.5) * block_levels(key_list[12], (D,), ((0, 4),), -0.4, 0.0), -0.5, 0.5).astype(jnp.bfloat16)
    gain_ffn_in = jnp.clip(jax.random.uniform(key_list[13], (D,), jnp.float32, -0.5, 0.5) * block_levels(key_list[13], (D,), ((0, 4),), -0.4, 0.0), -0.5, 0.5).astype(jnp.bfloat16)
    gain_ffn_out = jnp.clip(jax.random.uniform(key_list[14], (D,), jnp.float32, -0.5, 0.5) * block_levels(key_list[14], (D,), ((0, 4),), -0.4, 0.0), -0.5, 0.5).astype(jnp.bfloat16)
    return {"tokens": tokens, "cotangent": cotangent, "lengths": lengths, "block_order": block_order, "query_weight": query_weight, "key_weight": key_weight, "value_weight": value_weight, "out_weight": out_weight, "gate_weight": gate_weight, "up_weight": up_weight, "down_weight": down_weight, "gain_attn_in": gain_attn_in, "gain_attn_out": gain_attn_out, "gain_ffn_in": gain_ffn_in, "gain_ffn_out": gain_ffn_out}


@jax.custom_vjp
def low(v):
    return lax.optimization_barrier(v.astype(jnp.bfloat16)).astype(jnp.float32)

@jax.custom_vjp
def low_back(v):
    return v

def low_keep(v):
    return (low(v), None)

def low_pass(kept, grad):
    return (grad,)

def back_keep(v):
    return (v, None)

def back_low(kept, grad):
    return (low(grad),)
low.defvjp(low_keep, low_pass)
low_back.defvjp(back_keep, back_low)
cap_limit = 50.0
norm_eps = 1e-06
rope_base = 1000000.0
masked_value = -1000000000.0

def product(left, right):
    return jnp.dot(left, right, precision=lax.Precision.HIGHEST)

def normalize(values, gain):
    scale = lax.rsqrt(lax.optimization_barrier(jnp.mean(values * values, axis=-1, keepdims=True)) + norm_eps)
    return values * scale * (1.0 + gain)

def rotation_tables(positions):
    half_size = HD // 2
    freqs = rope_base ** (-(jnp.arange(half_size).astype(jnp.float32) * 2.0 / HD))
    angles = positions.astype(jnp.float32)[:, None] * freqs[None, :]
    return (jnp.cos(angles), jnp.sin(angles))

def rotate(values, cosine, sine_table):
    first_half = values[..., :HD // 2]
    second_half = values[..., HD // 2:]
    return jnp.concatenate([first_half * cosine - second_half * sine_table, second_half * cosine + first_half * sine_table], axis=-1)

def slot_positions(block_order):
    inner = jnp.arange(BLK, dtype=jnp.int32)
    return (block_order[:, None].astype(jnp.int32) * BLK + inner[None, :]).reshape(-1)

def sequence_layer(tokens, length, positions, params):
    query_weight, key_weight, value_weight, out_weight, gate_weight, up_weight, down_weight, gain_a, gain_b, gain_c, gain_d = params
    cosine, sine_table = rotation_tables(positions)
    normed = low(normalize(tokens, gain_a))
    query_pre = low_back(product(normed, query_weight)).reshape(SLOTS, H, HD)
    queries = low(rotate(query_pre, cosine[:, None, :], sine_table[:, None, :]) * HD ** (-0.5))
    key_rows = low(rotate(low_back(product(normed, key_weight)), cosine, sine_table))
    value_rows = low(low_back(product(normed, value_weight)))
    key_valid = positions < length
    query_rows = min(512, SLOTS)

    def attend(block):
        query_block, query_pos = block
        scores = low_back(jnp.einsum('qhd,kd->hqk', query_block, key_rows, precision=lax.Precision.HIGHEST))
        capped = cap_limit * jnp.tanh(scores / cap_limit)
        allowed = (positions[None, :] <= query_pos[:, None]) & key_valid[None, :]
        capped = jnp.where(allowed[None], capped, masked_value)
        row_top = lax.optimization_barrier(jnp.max(capped, axis=-1, keepdims=True))
        row_total = jnp.log(lax.optimization_barrier(jnp.sum(jnp.exp(capped - row_top), axis=-1, keepdims=True))) + row_top
        weights_soft = low(jnp.exp(capped - row_total))
        return jnp.einsum('hqk,kd->qhd', weights_soft, value_rows, precision=lax.Precision.HIGHEST)
    blocks = (queries.reshape(SLOTS // query_rows, query_rows, H, HD), positions.reshape(SLOTS // query_rows, query_rows))
    mixed = lax.map(jax.checkpoint(attend), blocks).reshape(SLOTS, H * HD)
    attended = low(low_back(mixed))
    branch = low_back(product(attended, out_weight))
    middle = tokens + normalize(branch, gain_b)
    second = low(normalize(middle, gain_c))
    gate_value = low_back(product(second, gate_weight))
    upward = low_back(product(second, up_weight))
    hidden = low(jax.nn.gelu(gate_value, approximate=True) * upward)
    output = low_back(product(hidden, down_weight))
    combined = middle + normalize(output, gain_d)
    return jnp.where(key_valid[:, None], combined, 0.0)

def forward(tokens, lengths, block_order, params):
    positions = slot_positions(block_order)
    flat_tokens = tokens.reshape(GROUPS * MB, SLOTS, D)
    flat_lengths = lengths.reshape(GROUPS * MB).astype(jnp.int32)

    def one_sequence(sequence_item):
        return sequence_layer(sequence_item[0], sequence_item[1], positions, params)
    outputs = lax.map(jax.checkpoint(one_sequence), (flat_tokens, flat_lengths))
    return outputs.reshape(GROUPS, MB, SLOTS, D)

def reference(tokens, cotangent, lengths, block_order, query_weight, key_weight, value_weight, out_weight, gate_weight, up_weight, down_weight, gain_attn_in, gain_attn_out, gain_ffn_in, gain_ffn_out):
    params = tuple((item.astype(jnp.float32) for item in (query_weight, key_weight, value_weight, out_weight, gate_weight, up_weight, down_weight, gain_attn_in, gain_attn_out, gain_ffn_in, gain_ffn_out)))

    def whole(tokens_in, *param_list):
        return forward(tokens_in, lengths, block_order, param_list)
    result, pullback = jax.vjp(whole, tokens.astype(jnp.float32), *params)
    grads = pullback(cotangent.astype(jnp.float32))
    return (result.astype(jnp.bfloat16), grads[0], grads[1], grads[2], grads[3], grads[4], grads[5], grads[6], grads[7], grads[8], grads[9], grads[10], grads[11])
```

```python
import functools

import jax
import jax.numpy as jnp
import numpy as np
from jax import lax
from jax.experimental import pallas as pl
from jax.experimental.pallas import tpu as pltpu
from jax.sharding import PartitionSpec as P

F32, BF16 = jnp.float32, jnp.bfloat16
CAP = 50.0
EPS = 1e-06
BASE = 1000000.0
HD = 256
HALF = HD // 2
BLK = 64
CHUNK = 512
AXES = ("ctx", "fsdp")
VMEM_LIMIT = 50 * 1024 * 1024


def all_places():
    for yl in range(2):
        for z in range(4):
            for x in range(4):
                for yh in range(2):
                    for c in range(2):
                        yield yl, z, x, yh, c


def flat(yl, z, x, yh, c):
    return (((yl * 4 + z) * 4 + x) * 2 + yh) * 2 + c


def send(array, move):
    pairs = [(flat(*p), flat(*move(*p))) for p in all_places()]
    return lax.ppermute(array, AXES, pairs)


def to_core(yl, z, x, yh, c):
    return yl, z, x, yh, 1 - c


def to_next(yl, z, x, yh, c):
    return 1 - yl, z, x, 1 - yh, c


def to_yl(yl, z, x, yh, c):
    return 1 - yl, z, x, yh, c


def to_yh(yl, z, x, yh, c):
    return yl, z, x, 1 - yh, c


def regroup(turn):
    def move(yl, z, x, yh, c):
        zh, zl, xh, xl = z // 2, z % 2, x // 2, x % 2
        return yl, c * 2 + zl, (xh ^ turn) * 2 + xl, yh, zh

    return move


def to_cube(step):
    dy, dz, dx = step >> 2, (step >> 1) & 1, step & 1

    def move(yl, z, x, yh, c):
        return yl ^ dy, z ^ dz, x ^ dx, yh, c

    return move


PLANE = [[yl * 16 + i for i in range(16)] for yl in range(2)]


def swap_plane(array):
    return lax.all_to_all(
        array, "ctx", split_axis=0, concat_axis=0, axis_index_groups=PLANE, tiled=True
    )


def inverse_rms(values):
    return lax.rsqrt(jnp.mean(values * values, axis=-1, keepdims=True) + EPS)


def norm_back(values, gain, grads):
    scale = inverse_rms(values)
    hat = values * scale
    scaled = grads * (1.0 + gain)
    inner = jnp.mean(scaled * hat, axis=-1, keepdims=True)
    return scale * (scaled - hat * inner), jnp.sum(grads * hat, axis=0)


def dot(left, right):
    return jnp.dot(left, right, preferred_element_type=F32)


def dot_nt(left, right):
    return lax.dot_general(left, right, (((1,), (1,)), ((), ())), preferred_element_type=F32)


def dot_tn(left, right):
    return lax.dot_general(left, right, (((0,), (0,)), ((), ())), preferred_element_type=F32)


def angle_tables():
    freqs = BASE ** (-(np.arange(HALF, dtype=np.float32) * 2.0 / HD)).astype(np.float32)
    coarse = (np.arange(64, dtype=np.float64) * 64)[:, None] * freqs[None, :].astype(np.float64)
    fine = np.arange(BLK, dtype=np.float64)[:, None] * freqs[None, :].astype(np.float64)
    tables = [np.cos(coarse), np.sin(coarse), np.cos(fine), np.sin(fine)]
    return np.stack(tables).astype(np.float32)


def chunk_tables(tables, chunk):
    rows = pl.ds(pl.multiple_of(chunk * 8, 8), 8)
    ca = tables[0, rows, :][:, None, :]
    sa = tables[1, rows, :][:, None, :]
    cb = tables[2][None]
    sb = tables[3][None]
    cosine = (ca * cb - sa * sb).reshape(CHUNK, HALF)
    sine = (sa * cb + ca * sb).reshape(CHUNK, HALF)
    return cosine, sine


def tile_facts(meta, t):
    b0, b1 = meta[72 + 2 * t], meta[73 + 2 * t]
    p0, p1 = meta[80 + 2 * t], meta[81 + 2 * t]
    length = meta[64]
    last = jnp.minimum(p1 * BLK + BLK, length)
    chunks = jnp.where(p0 * BLK < length, (last + CHUNK - 1) // CHUNK, 0)
    lane = lax.broadcasted_iota(jnp.int32, (1, 4 * BLK), 1)
    second = (lane // BLK) % 2 == 1
    limit = jnp.where(second, p1, p0) * BLK + lane % BLK
    return b0, b1, chunks, jnp.minimum(limit, length - 1)


def chunks_needed(meta):
    most = jnp.int32(0)
    for t in range(4):
        most = jnp.maximum(most, tile_facts(meta, t)[2])
    return most


def rows_of(chunk):
    return pl.ds(pl.multiple_of(chunk * CHUNK, CHUNK), CHUNK)


def tile_rows(ref, b0, b1):
    return jnp.concatenate([ref[0, b0], ref[0, b1], ref[1, b0], ref[1, b1]], axis=0)


def put_tile(ref, b0, b1, tile):
    ref[0, b0] = tile[0:BLK]
    ref[0, b1] = tile[BLK : 2 * BLK]
    ref[1, b0] = tile[2 * BLK : 3 * BLK]
    ref[1, b1] = tile[3 * BLK :]


def load_sorted(meta, pieces, sorted_ref, sem):
    for n, piece in enumerate(pieces):
        for b in range(4):
            at = pl.multiple_of(meta[n * 4 + b] * BLK, BLK)
            pltpu.make_async_copy(
                piece.at[pl.ds(b * BLK, BLK), :], sorted_ref.at[pl.ds(at, BLK), :], sem
            ).start()


def attend_kernel(meta, q_ref, w_ref, tables, *refs):
    pieces = refs[:16]
    o_ref, ot_ref, inv_ref, k_out, v_out = refs[16:21]
    normed, keys, values, values_t, acc, total, in_sem, k_sem, v_sem = refs[21:]
    load_sorted(meta, pieces, normed, in_sem)
    pltpu.make_async_copy(normed, normed, in_sem).wait()

    def prepare(chunk, carry):
        rows = rows_of(chunk)
        both = dot(normed[rows, :], w_ref[...])
        cosine, sine = chunk_tables(tables, chunk)
        first, second = both[:, :HALF], both[:, HALF:HD]
        keys[rows, :HALF] = (first * cosine - second * sine).astype(BF16)
        keys[rows, HALF:] = (second * cosine + first * sine).astype(BF16)
        low = both[:, HD:].astype(BF16)
        values[rows, :] = low
        values_t[chunk] = low.T
        return carry

    lax.fori_loop(0, chunks_needed(meta), prepare, 0)
    k_copy = pltpu.make_async_copy(keys, k_out, k_sem)
    v_copy = pltpu.make_async_copy(values, v_out, v_sem)
    k_copy.start()
    v_copy.start()

    def tile(t, carry):
        b0, b1, chunks, limit = tile_facts(meta, t)
        queries = tile_rows(q_ref, b0, b1)
        acc[...] = jnp.zeros_like(acc)
        total[...] = jnp.zeros_like(total)

        def step(chunk, inner):
            scores = dot_nt(keys[rows_of(chunk), :], queries)
            grown = jnp.exp(CAP * jnp.tanh(scores * (1.0 / CAP)))
            at = chunk * CHUNK + lax.broadcasted_iota(jnp.int32, (CHUNK, 4 * BLK), 0)
            grown = jnp.where(at <= limit, grown, 0.0)
            total[...] += jnp.sum(grown.reshape(CHUNK // 8, 8, 4 * BLK), axis=0)
            acc[...] += dot(values_t[chunk], grown.astype(BF16))
            return inner

        lax.fori_loop(0, chunks, step, 0)
        whole = jnp.sum(total[...], axis=0, keepdims=True)
        inverse = jnp.where(whole > 0.0, 1.0 / jnp.where(whole > 0.0, whole, 1.0), 0.0)
        mixed = acc[...] * inverse
        inv_ref[t] = jnp.broadcast_to(inverse, (8, 4 * BLK))
        ot_ref[t] = mixed.astype(BF16)
        put_tile(o_ref, b0, b1, mixed.T.astype(BF16))
        return carry

    lax.fori_loop(0, 4, tile, 0)
    k_copy.wait()
    v_copy.wait()


def attend_back_kernel(meta, q_ref, do_ref, ot_ref, inv_ref, k_ref, v_ref, tables, *refs):
    pieces = refs[:16]
    dq_ref, grad_ref, own_ref, oth_ref = refs[16:20]
    normed, keys_t, d_keys, d_values, d_both, acc, in_sem, out_sem = refs[20:]
    load_sorted(meta, pieces, normed, in_sem)
    needed = chunks_needed(meta)

    def prepare(chunk, carry):
        rows = rows_of(chunk)
        keys_t[chunk] = k_ref[rows, :].T
        d_keys[rows, :] = jnp.zeros((CHUNK, HD), F32)
        d_values[rows, :] = jnp.zeros((CHUNK, HD), F32)
        return carry

    lax.fori_loop(0, needed, prepare, 0)

    def tile(t, carry):
        b0, b1, chunks, limit = tile_facts(meta, t)
        queries = tile_rows(q_ref, b0, b1)
        grads = tile_rows(do_ref, b0, b1)
        inverse = inv_ref[t, 0:1, :]
        grads_t = grads.astype(F32).T
        center = jnp.sum(grads_t * ot_ref[t].astype(F32), axis=0, keepdims=True)
        acc[...] = jnp.zeros_like(acc)

        def step(chunk, inner):
            rows = rows_of(chunk)
            scores = dot_nt(k_ref[rows, :], queries)
            ratio = jnp.tanh(scores * (1.0 / CAP))
            probs = jnp.exp(CAP * ratio) * inverse
            at = chunk * CHUNK + lax.broadcasted_iota(jnp.int32, (CHUNK, 4 * BLK), 0)
            probs = jnp.where(at <= limit, probs, 0.0)
            d_probs = dot_nt(v_ref[rows, :], grads)
            d_scores = (probs * (d_probs - center) * (1.0 - ratio * ratio)).astype(BF16)
            d_values[rows, :] += dot(probs.astype(BF16), grads)
            d_keys[rows, :] += dot(d_scores, queries)
            acc[...] += dot(keys_t[chunk], d_scores)
            return inner

        lax.fori_loop(0, chunks, step, 0)
        put_tile(dq_ref, b0, b1, acc[...].T)
        return carry

    lax.fori_loop(0, 4, tile, 0)
    pltpu.make_async_copy(normed, normed, in_sem).wait()
    grad_ref[...] = jnp.zeros_like(grad_ref)

    def finish(chunk, carry):
        rows = rows_of(chunk)
        cosine, sine = chunk_tables(tables, chunk)
        first, second = d_keys[rows, :HALF], d_keys[rows, HALF:]
        d_both[rows, :HALF] = (first * cosine + second * sine).astype(BF16)
        d_both[rows, HALF:HD] = (second * cosine - first * sine).astype(BF16)
        d_both[rows, HD:] = d_values[rows, :].astype(BF16)
        grad_ref[...] += dot_tn(normed[rows, :], d_both[rows, :])
        return carry

    lax.fori_loop(0, needed, finish, 0)

    def clear(chunk, carry):
        d_both[rows_of(chunk), :] = jnp.zeros((CHUNK, 2 * HD), BF16)
        return carry

    lax.fori_loop(needed, 8, clear, 0)
    for n in range(16):
        target = own_ref if n < 8 else oth_ref
        for b in range(4):
            at = pl.multiple_of(meta[n * 4 + b] * BLK, BLK)
            pltpu.make_async_copy(
                d_both.at[pl.ds(at, BLK), :], target.at[n % 8, pl.ds(b * BLK, BLK), :], out_sem
            ).start()
    pltpu.make_async_copy(d_both, d_both, out_sem).wait()


SMEM_SPEC = pl.BlockSpec(memory_space=pltpu.SMEM)
VMEM_SPEC = pl.BlockSpec(memory_space=pltpu.VMEM)
ANY_SPEC = pl.BlockSpec(memory_space=pl.ANY)
SLOTS = 4096


def attend(meta, queries, key_value_weight, tables, pieces):
    width = pieces[0].shape[1]
    return pl.pallas_call(
        attend_kernel,
        out_shape=(
            jax.ShapeDtypeStruct((2, 8, BLK, HD), BF16),
            jax.ShapeDtypeStruct((4, HD, 4 * BLK), BF16),
            jax.ShapeDtypeStruct((4, 8, 4 * BLK), F32),
            jax.ShapeDtypeStruct((SLOTS, HD), BF16),
            jax.ShapeDtypeStruct((SLOTS, HD), BF16),
        ),
        in_specs=[SMEM_SPEC, VMEM_SPEC, VMEM_SPEC, VMEM_SPEC] + [ANY_SPEC] * 16,
        out_specs=(VMEM_SPEC, VMEM_SPEC, VMEM_SPEC, ANY_SPEC, ANY_SPEC),
        scratch_shapes=[
            pltpu.VMEM((SLOTS, width), BF16),
            pltpu.VMEM((SLOTS, HD), BF16),
            pltpu.VMEM((SLOTS, HD), BF16),
            pltpu.VMEM((SLOTS // CHUNK, HD, CHUNK), BF16),
            pltpu.VMEM((HD, 4 * BLK), F32),
            pltpu.VMEM((8, 4 * BLK), F32),
            pltpu.SemaphoreType.DMA,
            pltpu.SemaphoreType.DMA,
            pltpu.SemaphoreType.DMA,
        ],
        compiler_params=pltpu.CompilerParams(vmem_limit_bytes=VMEM_LIMIT),
        cost_estimate=pl.CostEstimate(
            flops=8 * 10**9, bytes_accessed=16 * 10**6, transcendentals=8 * 10**6
        ),
        name="attend",
    )(meta, queries, key_value_weight, tables, *pieces)


def attend_back(meta, queries, d_attended, mixed_t, inverse, keys, values, tables, pieces):
    width = pieces[0].shape[1]
    return pl.pallas_call(
        attend_back_kernel,
        out_shape=(
            jax.ShapeDtypeStruct((2, 8, BLK, HD), F32),
            jax.ShapeDtypeStruct((width, 2 * HD), F32),
            jax.ShapeDtypeStruct((8, 4 * BLK, 2 * HD), BF16),
            jax.ShapeDtypeStruct((8, 4 * BLK, 2 * HD), BF16),
        ),
        in_specs=[SMEM_SPEC] + [VMEM_SPEC] * 7 + [ANY_SPEC] * 16,
        out_specs=(VMEM_SPEC, VMEM_SPEC, ANY_SPEC, ANY_SPEC),
        scratch_shapes=[
            pltpu.VMEM((SLOTS, width), BF16),
            pltpu.VMEM((SLOTS // CHUNK, HD, CHUNK), BF16),
            pltpu.VMEM((SLOTS, HD), F32),
            pltpu.VMEM((SLOTS, HD), F32),
            pltpu.VMEM((SLOTS, 2 * HD), BF16),
            pltpu.VMEM((HD, 4 * BLK), F32),
            pltpu.SemaphoreType.DMA,
            pltpu.SemaphoreType.DMA,
        ],
        compiler_params=pltpu.CompilerParams(vmem_limit_bytes=VMEM_LIMIT),
        cost_estimate=pl.CostEstimate(
            flops=20 * 10**9, bytes_accessed=24 * 10**6, transcendentals=8 * 10**6
        ),
        name="attend_back",
    )(meta, queries, d_attended, mixed_t, inverse, keys, values, tables, *pieces)


def sum_shards(own, other):
    rows, cols = own.shape
    both = jnp.concatenate([own, other], axis=1).astype(BF16)
    got = swap_plane(both.reshape(16, rows // 16, 2 * cols))
    part = jnp.sum(got.astype(F32), axis=0).astype(BF16)
    mine, theirs = part[:, :cols], part[:, cols:]
    total = (
        mine.astype(F32)
        + send(mine, to_yl).astype(F32)
        + send(theirs, to_next).astype(F32)
        + send(theirs, to_yh).astype(F32)
    ).astype(BF16)
    everyone = swap_plane(jnp.broadcast_to(total[None], (16, rows // 16, cols)))
    return everyone.reshape(rows, cols)


def on_device(
    tokens,
    cotangent,
    lengths,
    block_order,
    query_weight,
    key_weight,
    value_weight,
    out_weight,
    gate_weight,
    up_weight,
    down_weight,
    gain_attn_in,
    gain_attn_out,
    gain_ffn_in,
    gain_ffn_out,
):
    ctx, fsdp = lax.axis_index("ctx"), lax.axis_index("fsdp")
    yl, z, x = ctx // 16, (ctx // 4) % 4, ctx % 4
    yh, c = fsdp // 2, fsdp % 2
    zh, zl, xh, xl = z // 2, z % 2, x // 2, x % 2
    low_y, low_c, low_x = yh == 0, c == 0, xh == 0
    own_rows = 4 * BLK
    width = tokens.shape[-1]

    def gather_rows(array):
        pieces = (
            send(jnp.where(low_x, array[0, 0], array[0, 1]), regroup(0)),
            send(jnp.where(low_x, array[0, 1], array[0, 0]), regroup(1)),
        )
        return jnp.concatenate(pieces, axis=0)

    def return_rows(rows):
        first = send(rows[: own_rows // 2], regroup(0))
        second = send(rows[own_rows // 2 :], regroup(1))
        return jnp.stack([jnp.where(low_x, first, second), jnp.where(low_x, second, first)])[None]

    rows_in = gather_rows(tokens)

    gains = jnp.stack([gain_attn_in, gain_attn_out, gain_ffn_in, gain_ffn_out])
    gains_next = send(gains, to_next)
    half_gains = jnp.stack(
        [jnp.where(low_y, gains, gains_next), jnp.where(low_y, gains_next, gains)]
    )
    half_other = send(half_gains, to_core)
    quarters = jnp.stack(
        [jnp.where(low_c, half_gains, half_other), jnp.where(low_c, half_other, half_gains)], axis=1
    )
    all_gains = jnp.transpose(quarters, (2, 0, 1, 3)).reshape(4, width).astype(F32)
    gain_a, gain_b, gain_c, gain_d = (all_gains[i] for i in range(4))

    lengths_other = send(lengths, to_core)
    lengths_here = jnp.where(zh == c, lengths, lengths_other)
    length = jnp.where(low_x, lengths_here[0, 0], lengths_here[0, 1])

    qkv_own = jnp.concatenate([query_weight, key_weight, value_weight], axis=1)
    qkv_next = send(qkv_own, to_next)
    heads = HD
    kv_low = jnp.where(low_y, qkv_own[:, heads:], qkv_next[:, heads:])
    kv_high = jnp.where(low_y, qkv_next[:, heads:], qkv_own[:, heads:])
    kv_pair = jnp.stack([kv_low, kv_high])
    kv_pair_other = send(kv_pair, to_core)
    kv_c0 = jnp.where(low_c, kv_pair, kv_pair_other)
    kv_c1 = jnp.where(low_c, kv_pair_other, kv_pair)
    quarter = key_weight.shape[1]
    kv_weight = jnp.concatenate(
        [m[:, :quarter] for m in (kv_c0[0], kv_c1[0], kv_c0[1], kv_c1[1])]
        + [m[:, quarter:] for m in (kv_c0[0], kv_c1[0], kv_c0[1], kv_c1[1])],
        axis=1,
    )
    q_own, q_next = qkv_own[:, :heads], qkv_next[:, :heads]

    do_own = jnp.concatenate([down_weight, out_weight], axis=0)
    do_next = send(do_own, to_next)
    gu_own = jnp.concatenate([gate_weight, up_weight], axis=1)
    gu_next = send(gu_own, to_next)
    hidden_cols = gate_weight.shape[1]
    down_own, out_own = do_own[:hidden_cols], do_own[hidden_cols:]
    down_next, out_next = do_next[:hidden_cols], do_next[hidden_cols:]

    stored = []
    for other in range(2):
        for step in range(8):
            dy, dz, dx = step >> 2, (step >> 1) & 1, step & 1
            for turn in range(2):
                place = (yl ^ dy) * 16 + ((c ^ other) * 2 + (zl ^ dz)) * 4
                place = place + (xh ^ turn) * 2 + (xl ^ dx)
                stored += [place * 2, place * 2 + 1]
    stored = jnp.stack(stored)
    slots = jnp.arange(64, dtype=jnp.int32)
    block_at = jnp.sum(
        jnp.where(stored[:, None] == slots[None, :], block_order[None, :], 0), axis=1
    ).astype(jnp.int32)
    q_blocks = jnp.concatenate([block_at[0:4], block_at[32:36]])
    rank = jnp.sum((q_blocks[None, :] < q_blocks[:, None]).astype(jnp.int32), axis=1)
    eight = jnp.arange(8, dtype=jnp.int32)
    chosen = rank[None, :] == eight[:, None]
    order = jnp.sum(jnp.where(chosen, eight[None, :], 0), axis=1).astype(jnp.int32)
    order_block = jnp.sum(jnp.where(chosen, q_blocks[None, :], 0), axis=1).astype(jnp.int32)
    meta = jnp.concatenate(
        [block_at, jnp.full((8,), length, jnp.int32), order, order_block]
    )
    row_pos = (q_blocks[:, None] * BLK + jnp.arange(BLK, dtype=jnp.int32)[None, :]).reshape(-1)
    valid = (row_pos[:own_rows] < length)[:, None]

    start = rows_in.astype(F32)
    normed_own = (start * inverse_rms(start) * (1.0 + gain_a)).astype(BF16)
    near = [normed_own] + [send(normed_own, to_cube(step)) for step in range(1, 8)]
    far = [send(piece, to_core) for piece in near]
    pieces = near + far
    normed = jnp.concatenate([near[0], far[0]], axis=0)

    freqs = BASE ** (-(jnp.arange(HALF).astype(F32) * 2.0 / HD))
    angles = row_pos.astype(F32)[:, None] * freqs[None, :]
    cosine, sine = jnp.cos(angles), jnp.sin(angles)

    def rotated(pre):
        first, second = pre[:, :HALF], pre[:, HALF:]
        turned = jnp.concatenate(
            [first * cosine - second * sine, second * cosine + first * sine], axis=1
        )
        return (turned * HD ** (-0.5)).astype(BF16)

    queries = jnp.stack([rotated(dot(normed, q_own)), rotated(dot(normed, q_next))])
    queries = queries.reshape(2, 8, BLK, HD)
    tables = jnp.asarray(angle_tables())
    mixed, mixed_t, inverse, keys, values = attend(meta, queries, kv_weight, tables, pieces)
    mixed = mixed.reshape(2, 2 * own_rows, HD)

    def share(partial):
        return partial[:own_rows] + send(partial[own_rows:].astype(BF16), to_core).astype(F32)

    def both_cores(rows):
        return jnp.concatenate([rows, send(rows, to_core)], axis=0)

    branch = share(dot(mixed[0], out_own) + dot(mixed[1], out_next))
    middle = start + branch * inverse_rms(branch) * (1.0 + gain_b)
    second = both_cores((middle * inverse_rms(middle) * (1.0 + gain_c)).astype(BF16))

    def gelu_product(gate_up):
        return jax.nn.gelu(gate_up[:, :hidden_cols], approximate=True) * gate_up[:, hidden_cols:]

    gate_up_own, gate_up_next = dot(second, gu_own), dot(second, gu_next)
    hidden_own, pull_own = jax.vjp(gelu_product, gate_up_own)
    hidden_next, pull_next = jax.vjp(gelu_product, gate_up_next)
    hidden_own, hidden_next = hidden_own.astype(BF16), hidden_next.astype(BF16)
    output = share(dot(hidden_own, down_own) + dot(hidden_next, down_next))
    result = jnp.where(valid, middle + output * inverse_rms(output) * (1.0 + gain_d), 0.0)
    result_block = return_rows(result.astype(BF16))

    seed = jnp.where(valid, gather_rows(cotangent).astype(F32), 0.0)
    d_output, d_gain_d = norm_back(output, gain_d, seed)
    d_output = both_cores(d_output.astype(BF16))
    d_gu_own = pull_own(dot_nt(d_output, down_own))[0].astype(BF16)
    d_gu_next = pull_next(dot_nt(d_output, down_next))[0].astype(BF16)
    d_second = share(dot_nt(d_gu_own, gu_own) + dot_nt(d_gu_next, gu_next))
    d_mid, d_gain_c = norm_back(middle, gain_c, d_second)
    d_middle = seed + d_mid
    d_branch, d_gain_b = norm_back(branch, gain_b, d_middle)
    d_branch = both_cores(d_branch.astype(BF16))
    d_mixed = jnp.stack([dot_nt(d_branch, out_own), dot_nt(d_branch, out_next)]).astype(BF16)

    grads_own = jnp.concatenate(
        [dot_tn(second, d_gu_own), dot_tn(d_output, hidden_own), dot_tn(d_branch, mixed[0])], axis=1
    )
    grads_next = jnp.concatenate(
        [dot_tn(second, d_gu_next), dot_tn(d_output, hidden_next), dot_tn(d_branch, mixed[1])], axis=1
    )
    ffn_sum = sum_shards(grads_own, grads_next)

    d_queries, kv_grad, d_near, d_far = attend_back(
        meta,
        queries,
        d_mixed.reshape(2, 8, BLK, HD),
        mixed_t,
        inverse,
        keys,
        values,
        tables,
        pieces,
    )
    chip_sum = (d_near.astype(F32) + send(d_far, to_core).astype(F32)).astype(BF16)
    d_kv = chip_sum[0].astype(F32)
    for step in range(1, 8):
        d_kv = d_kv + send(chip_sum[step], to_cube(step)).astype(F32)
    d_kv = d_kv.astype(BF16)

    def unrotated(turned):
        scaled = turned.reshape(2 * own_rows, HD) * HD ** (-0.5)
        first, second = scaled[:, :HALF], scaled[:, HALF:]
        return jnp.concatenate(
            [first * cosine + second * sine, second * cosine - first * sine], axis=1
        ).astype(BF16)

    d_q_own, d_q_next = unrotated(d_queries[0]), unrotated(d_queries[1])
    d_normed = share(dot_nt(d_q_own, q_own) + dot_nt(d_q_next, q_next))
    d_normed = d_normed + dot_nt(d_kv, kv_weight)
    d_start, _ = norm_back(start, gain_a, d_normed)
    token_block = return_rows((d_middle + d_start).astype(BF16)).astype(F32)

    q_grad_own, q_grad_next = dot_tn(normed, d_q_own), dot_tn(normed, d_q_next)
    split = kv_grad.reshape(width, 2, 2, 2, quarter)
    keep = jnp.where(low_c, split[:, :, :, 0], split[:, :, :, 1])
    give = jnp.where(low_c, split[:, :, :, 1], split[:, :, :, 0])
    keep = keep + send(give.astype(BF16), to_core).astype(F32)
    kv_grad_own = jnp.where(low_y, keep[:, :, 0], keep[:, :, 1]).reshape(width, 2 * quarter)
    kv_grad_next = jnp.where(low_y, keep[:, :, 1], keep[:, :, 0]).reshape(width, 2 * quarter)
    qkv_grad_own = jnp.concatenate([q_grad_own, kv_grad_own], axis=1)
    qkv_grad_next = jnp.concatenate([q_grad_next, kv_grad_next], axis=1)
    d_gain_a = jnp.sum(qkv_own.astype(F32) * qkv_grad_own, axis=1)
    d_gain_a = d_gain_a + jnp.sum(qkv_next.astype(F32) * qkv_grad_next, axis=1)
    d_gain_a = d_gain_a / (1.0 + gain_a)
    d_gains = jnp.stack([d_gain_a, d_gain_b, d_gain_c, d_gain_d])
    d_gains = (d_gains + send(d_gains.astype(BF16), to_core).astype(F32)).T
    qkv_sum = sum_shards(
        jnp.concatenate([qkv_grad_own, d_gains], axis=1),
        jnp.concatenate([qkv_grad_next, d_gains], axis=1),
    ).astype(F32)
    share_rows = width // 4
    gain_grads = lax.dynamic_slice_in_dim(qkv_sum[:, -4:], fsdp * share_rows, share_rows, axis=0)
    ffn_sum = ffn_sum.astype(F32)
    at_v = heads + quarter
    return (
        result_block,
        token_block,
        qkv_sum[:, :heads],
        qkv_sum[:, heads:at_v],
        qkv_sum[:, at_v : at_v + quarter],
        ffn_sum[:, 3 * hidden_cols :].T,
        ffn_sum[:, :hidden_cols],
        ffn_sum[:, hidden_cols : 2 * hidden_cols],
        ffn_sum[:, 2 * hidden_cols : 3 * hidden_cols].T,
        gain_grads[:, 0],
        gain_grads[:, 1],
        gain_grads[:, 2],
        gain_grads[:, 3],
    )


def solution(mesh):
    rows, cols, first = P("fsdp", None, "ctx", None), P(None, "fsdp"), P("fsdp", None)
    weights = (cols, cols, cols, first, cols, cols, first)
    gains = (P("fsdp"),) * 4
    return jax.shard_map(
        on_device,
        mesh=mesh,
        in_specs=(rows, rows, first, P()) + weights + gains,
        out_specs=(rows, rows) + weights + gains,
        check_vma=False,
    )
```

```python
import functools

import jax
import jax.numpy as jnp
import numpy as np
from jax import lax
from jax.experimental import pallas as pl
from jax.experimental.pallas import tpu as pltpu
from jax.sharding import PartitionSpec as P

F32, BF16 = jnp.float32, jnp.bfloat16
CAP = 50.0
EPS = 1e-06
BASE = 1000000.0
HD = 256
HALF = HD // 2
BLK = 64
CHUNK = 512
VMEM = 54
AXES = ("ctx", "fsdp")


def all_places():
    for yl in range(2):
        for z in range(4):
            for x in range(4):
                for yh in range(2):
                    for c in range(2):
                        yield yl, z, x, yh, c


def flat(yl, z, x, yh, c):
    return (((yl * 4 + z) * 4 + x) * 2 + yh) * 2 + c


def send(array, move):
    pairs = [(flat(*p), flat(*move(*p))) for p in all_places()]
    return lax.ppermute(array, AXES, pairs)


def to_core(yl, z, x, yh, c):
    return yl, z, x, yh, 1 - c


def to_next(yl, z, x, yh, c):
    return 1 - yl, z, x, 1 - yh, c


def to_yl(yl, z, x, yh, c):
    return 1 - yl, z, x, yh, c


def to_yh(yl, z, x, yh, c):
    return yl, z, x, 1 - yh, c


def to_zpair(yl, z, x, yh, c):
    return yl, z ^ 1, x, yh, c


def to_xpair(yl, z, x, yh, c):
    return yl, z, x ^ 1, yh, c


def to_zring(yl, z, x, yh, c):
    return yl, (z + (1 if z % 2 else 3)) % 4, x, yh, c


def to_xring(yl, z, x, yh, c):
    return yl, z, (x + (1 if x % 2 else 3)) % 4, yh, c


def regroup(turn):
    def move(yl, z, x, yh, c):
        zh, zl, xh, xl = z // 2, z % 2, x // 2, x % 2
        return yl, c * 2 + zl, (xh ^ turn) * 2 + xl, yh, zh

    return move


def to_cube(step):
    dy, dz, dx = step >> 2, (step >> 1) & 1, step & 1

    def move(yl, z, x, yh, c):
        return yl ^ dy, z ^ dz, x ^ dx, yh, c

    return move


PARTS = ((0, 96, (4, 2, 1)), (96, 176, (2, 1, 4)), (176, 256, (1, 4, 2)))


BACK_PARTS = ((0, 128, (4, 2, 1)), (128, 256, (2, 1, 4)))


def held_by(order):
    a, b, d = order
    low = (0, a, b, a | b)
    return low, tuple(d | step for step in low)


def copy_kernel(array, out):
    out[...] = array[...]


def pack_rows_kernel(first, second, out):
    out[: first.shape[0]] = first[...]
    out[first.shape[0] :] = second[...]


def pack_columns_kernel(first, second, out):
    out[:, : first.shape[1]] = first[...]
    out[:, first.shape[1] :] = second[...]


def pack_qkv_kernel(query, key_t, value_t, gains, out):
    rows, width = query.shape[0], gains.shape[1]
    out[:rows, :HD] = query[...]
    out[:rows, HD:] = jnp.concatenate([key_t[...], value_t[...]], axis=0).T
    out[rows:, :] = jnp.zeros((out.shape[0] - rows, out.shape[1]), BF16)
    out[rows : rows + gains.shape[0], :width] = gains[...]


def kv_pair_kernel(spot, own, after, out):
    low = spot[0] == 0
    half = HD // 2
    rows = own.shape[0] - 16
    mine, theirs = own[:rows, HD:], after[:rows, HD:]
    out[:rows, :half] = jnp.where(low, mine, theirs)
    out[:rows, half:] = jnp.where(low, theirs, mine)
    mine, theirs = own[rows:, :HD], after[rows:, :HD]
    out[rows : rows + 16, :] = jnp.where(low, mine, theirs)
    out[rows + 16 :, :] = jnp.where(low, theirs, mine)


def pick_kernel(spot, array, first, second):
    low = spot[4] == 0
    first[...] = jnp.where(low, array[0], array[1])
    second[...] = jnp.where(low, array[1], array[0])


def sizes():
    return [last - first for first, last, order in PARTS]


def cut_kernel(r0, r1, *outs):
    half = r0.shape[0]
    for (first, last, order), out in zip(PARTS, outs):
        if first < half:
            out[: min(last, half) - first] = r0[first : min(last, half)]
        if last > half:
            out[max(first, half) - first :] = r1[max(first, half) - half : last - half]


def join_kernel(count, *refs):
    ins, outs = refs[: 2 * count], refs[-count:]
    for p in range(count):
        rows = ins[p].shape[0]
        outs[p][:rows] = ins[p][...]
        outs[p][rows:] = ins[count + p][...]


def join_all_kernel(*refs):
    ins, outs = refs[:6], refs[-4:]
    at = 0
    for p in range(3):
        rows = ins[p].shape[0]
        outs[p][:rows] = ins[p][...]
        outs[p][rows:] = ins[3 + p][...]
        outs[3][at : at + rows] = ins[p][...]
        outs[3][at + rows : at + 2 * rows] = ins[3 + p][...]
        at += 2 * rows


PLANE = [[yl * 16 + i for i in range(16)] for yl in range(2)]


def swap_plane(array):
    return lax.all_to_all(
        array, "ctx", split_axis=0, concat_axis=0, axis_index_groups=PLANE, tiled=True
    )


def along_x(shift):
    def move(yl, z, x, yh, c):
        return yl, z, (x + shift) % 4, yh, c

    return move


def along_z(shift):
    def move(yl, z, x, yh, c):
        return yl, (z + shift) % 4, x, yh, c

    return move


def spread(arrays, along):
    return [send(array, along(r + 1)) for r, array in enumerate(arrays)]


COLUMNS = [[yl * 16 + z * 4 + x for z in range(4)] for yl in range(2) for x in range(4)]


def swap_z(array):
    return lax.all_to_all(
        array, "ctx", split_axis=0, concat_axis=0, axis_index_groups=COLUMNS, tiled=True
    )


def inverse_rms(values):
    return lax.rsqrt(jnp.mean(values * values, axis=-1, keepdims=True) + EPS)


def norm_back(values, gain, grads):
    scale = inverse_rms(values)
    hat = values * scale
    scaled = grads * (1.0 + gain)
    inner = jnp.mean(scaled * hat, axis=-1, keepdims=True)
    return scale * (scaled - hat * inner), jnp.sum(grads * hat, axis=0)


def dot(left, right):
    return jnp.dot(left, right, preferred_element_type=F32)


def dot_nt(left, right):
    return lax.dot_general(left, right, (((1,), (1,)), ((), ())), preferred_element_type=F32)


def dot_tn(left, right):
    return lax.dot_general(left, right, (((0,), (0,)), ((), ())), preferred_element_type=F32)


def angle_tables():
    freqs = BASE ** (-(np.arange(HALF, dtype=np.float32) * 2.0 / HD)).astype(np.float32)
    coarse = (np.arange(64, dtype=np.float64) * 64)[:, None] * freqs[None, :].astype(np.float64)
    fine = np.arange(BLK, dtype=np.float64)[:, None] * freqs[None, :].astype(np.float64)
    tables = [np.cos(coarse), np.sin(coarse), np.cos(fine), np.sin(fine)]
    return np.stack(tables).astype(np.float32)


SMEM_SPEC = pl.BlockSpec(memory_space=pltpu.SMEM)
VMEM_SPEC = pl.BlockSpec(memory_space=pltpu.VMEM)
ANY_SPEC = pl.BlockSpec(memory_space=pl.ANY)
HBM_SPEC = pl.BlockSpec(memory_space=pltpu.HBM)
DMA = pltpu.SemaphoreType.DMA
SLOTS = 4096


def shape(dims, dtype):
    return jax.ShapeDtypeStruct(dims, dtype)


def cost(gflops, mbytes):
    return pl.CostEstimate(
        flops=int(gflops * 10**9), bytes_accessed=int(mbytes * 10**6), transcendentals=0
    )


def params(mbytes):
    return pltpu.CompilerParams(vmem_limit_bytes=mbytes * 1024 * 1024)


def step(kernel, outs, arrays, after=(), meta=None, mbytes=VMEM, name=None, scratch=()):
    scalars = 0 if meta is None else 1
    used = scalars + len(arrays)

    def body(*refs):
        kernel(*refs[:used], *refs[used + len(after) :])

    return pl.pallas_call(
        body,
        out_shape=tuple(outs),
        in_specs=[SMEM_SPEC] * scalars + [VMEM_SPEC] * len(arrays) + [ANY_SPEC] * len(after),
        out_specs=(VMEM_SPEC,) * len(outs),
        scratch_shapes=list(scratch),
        compiler_params=params(mbytes),
        cost_estimate=cost(0.1, 4),
        name=name,
    )(*(() if meta is None else (meta,)), *arrays, *after)


def gate_kernel(*refs):
    pass


def gate(arrays, after):
    return pl.pallas_call(
        gate_kernel,
        out_shape=tuple(shape(a.shape, a.dtype) for a in arrays),
        in_specs=[ANY_SPEC] * (len(arrays) + len(after)),
        out_specs=(ANY_SPEC,) * len(arrays),
        input_output_aliases={i: i for i in range(len(arrays))},
        name="gate",
    )(*arrays, *after)


def chunk_tables(tables, chunk):
    rows = pl.ds(pl.multiple_of(chunk * 8, 8), 8)
    ca = tables[0, rows, :][:, None, :]
    sa = tables[1, rows, :][:, None, :]
    cb = tables[2][None]
    sb = tables[3][None]
    cosine = (ca * cb - sa * sb).reshape(CHUNK, HALF)
    sine = (sa * cb + ca * sb).reshape(CHUNK, HALF)
    return cosine, sine


def block_tables(tables, block):
    ca, sa = tables[0, pl.ds(block, 1), :], tables[1, pl.ds(block, 1), :]
    cb, sb = tables[2], tables[3]
    return ca * cb - sa * sb, sa * cb + ca * sb


def tile_facts(meta, t):
    b0, b1 = meta[72 + 2 * t], meta[73 + 2 * t]
    p0, p1 = meta[80 + 2 * t], meta[81 + 2 * t]
    length = meta[64]
    last = jnp.minimum(p1 * BLK + BLK, length)
    chunks = jnp.where(p0 * BLK < length, (last + CHUNK - 1) // CHUNK, 0)
    lane = lax.broadcasted_iota(jnp.int32, (1, 4 * BLK), 1)
    second = (lane // BLK) % 2 == 1
    limit = jnp.where(second, p1, p0) * BLK + lane % BLK
    return b0, b1, chunks, jnp.minimum(limit, length - 1)


def chunks_needed(meta):
    most = jnp.int32(0)
    for t in range(4):
        most = jnp.maximum(most, tile_facts(meta, t)[2])
    return most


def q_block(meta, b):
    return meta[b] if b < 4 else meta[28 + b]


def rows_of(chunk):
    return pl.ds(pl.multiple_of(chunk * CHUNK, CHUNK), CHUNK)


def block_rows(block):
    return pl.ds(pl.multiple_of(block * BLK, BLK), BLK)


def tile_rows(ref, b0, b1):
    return jnp.concatenate([ref[0, b0], ref[0, b1], ref[1, b0], ref[1, b1]], axis=0)


def put_tile(own, oth, b0, b1, tile):
    for block, rows in ((b0, 0), (b1, BLK)):
        for ref, base in ((own, 0), (oth, 4)):

            @pl.when((block >= base) & (block < base + 4))
            def _():
                to = pl.ds(pl.multiple_of((block - base) * BLK, BLK), BLK)
                ref[0, to, :] = tile[rows : rows + BLK]
                ref[1, to, :] = tile[2 * BLK + rows : 3 * BLK + rows]


def attend_kernel(after, meta, q_own, qkv_next, kv_mine, kv_theirs, gains, tables, *refs):
    q_ref, own_ref, oth_ref, ot_ref, inv_ref, w_ref, n_out, k_out, v_out = refs[10 + after : 19 + after]
    normed, normed_q, keys, values, values_t, acc, total, in_sem, n_sem, k_sem, v_sem = refs[19 + after :]
    for core in range(2):
        for p, (first, last, order) in enumerate(PARTS):
            size = last - first
            for half, steps in enumerate(held_by(order)):
                source, base = refs[half * 3 + p], 0
                if core == 1:
                    source = refs[6] if half == 0 else refs[7 + p]
                    base = 4 * first if half == 0 else 0
                for i, step in enumerate(steps):
                    row = first
                    while row < last:
                        block, inner = row // BLK, row % BLK
                        count = min(last - row, BLK - inner)
                        to = pl.multiple_of(meta[(core * 8 + step) * 4 + block] * BLK + inner, 16)
                        pltpu.make_async_copy(
                            source.at[pl.ds(base + i * size + row - first, count), :],
                            normed.at[pl.ds(to, count), :],
                            in_sem,
                        ).start()
                        row += count
    low = meta[66] == 0
    rows = w_ref.shape[0]
    first_core = jnp.where(low, kv_mine[:rows], kv_theirs[:rows])
    second_core = jnp.where(low, kv_theirs[:rows], kv_mine[:rows])
    quarter = HD // 4
    for kv in range(2):
        for side in range(2):
            at = side * 2 * quarter + kv * quarter
            to = kv * HD + side * 2 * quarter
            w_ref[:, to : to + 2 * quarter] = jnp.concatenate(
                [first_core[:, at : at + quarter], second_core[:, at : at + quarter]], axis=1
            )
    pltpu.make_async_copy(normed, normed, in_sem).wait()

    def prepare(chunk, carry):
        rows = rows_of(chunk)
        start = normed[rows, :].astype(F32)
        low_rows = (start * inverse_rms(start) * (1.0 + gains[0:1, :])).astype(BF16)
        normed[rows, :] = low_rows
        both = dot(low_rows, w_ref[...])
        cosine, sine = chunk_tables(tables, chunk)
        first, second = both[:, :HALF], both[:, HALF:HD]
        keys[rows, :HALF] = (first * cosine - second * sine).astype(BF16)
        keys[rows, HALF:] = (second * cosine + first * sine).astype(BF16)
        low = both[:, HD:].astype(BF16)
        values[rows, :] = low
        values_t[chunk] = low.T
        return carry

    lax.fori_loop(0, chunks_needed(meta), prepare, 0)
    copies = [
        pltpu.make_async_copy(normed, n_out, n_sem),
        pltpu.make_async_copy(keys, k_out, k_sem),
        pltpu.make_async_copy(values, v_out, v_sem),
    ]
    for copy in copies:
        copy.start()
    for b in range(8):
        normed_q[b * BLK : (b + 1) * BLK, :] = normed[block_rows(q_block(meta, b)), :]
    for h, weight in enumerate((q_own[...], qkv_next[: q_own.shape[0], :HD])):
        pre = dot(normed_q[...], weight) * HD ** (-0.5)
        for b in range(8):
            cosine, sine = block_tables(tables, q_block(meta, b))
            first = pre[b * BLK : (b + 1) * BLK, :HALF]
            second = pre[b * BLK : (b + 1) * BLK, HALF:]
            q_ref[h, b, :, :HALF] = (first * cosine - second * sine).astype(BF16)
            q_ref[h, b, :, HALF:] = (second * cosine + first * sine).astype(BF16)

    def tile(t, carry):
        b0, b1, chunks, limit = tile_facts(meta, t)
        queries = tile_rows(q_ref, b0, b1)
        acc[...] = jnp.zeros_like(acc)
        total[...] = jnp.zeros_like(total)

        def step(chunk, inner):
            scores = dot_nt(keys[rows_of(chunk), :], queries)
            grown = jnp.exp(CAP * jnp.tanh(scores * (1.0 / CAP)))
            at = chunk * CHUNK + lax.broadcasted_iota(jnp.int32, (CHUNK, 4 * BLK), 0)
            grown = jnp.where(at <= limit, grown, 0.0)
            total[...] += jnp.sum(grown.reshape(CHUNK // 8, 8, 4 * BLK), axis=0)
            acc[...] += dot(values_t[chunk], grown.astype(BF16))
            return inner

        lax.fori_loop(0, chunks, step, 0)
        whole = jnp.sum(total[...], axis=0, keepdims=True)
        inverse = jnp.where(whole > 0.0, 1.0 / jnp.where(whole > 0.0, whole, 1.0), 0.0)
        mixed = acc[...] * inverse
        inv_ref[t] = jnp.broadcast_to(inverse, (8, 4 * BLK))
        ot_ref[t] = mixed.astype(BF16)
        put_tile(own_ref, oth_ref, b0, b1, mixed.T.astype(BF16))
        return carry

    lax.fori_loop(0, 4, tile, 0)
    for copy in copies:
        copy.wait()


def attend_back_kernel(
    meta, q_ref, do_own, pack_oth, ot_ref, inv_ref, q_own, qkv_next, kv_w, gains, gain_in, tables, k_in, v_in, n_in, feed_terms,
    terms_ref, give_ref, dn_own, dn_give, near_ref, far_ref, *refs
):
    do_ref, do_oth, normed, k_ref, v_ref, normed_q, dq, kv_grad, keys_t, d_keys, d_values, d_both, acc, do_sem, k_sem, v_sem, in_sem, out_sem = refs
    loads = [
        pltpu.make_async_copy(k_in, k_ref, k_sem),
        pltpu.make_async_copy(v_in, v_ref, v_sem),
        pltpu.make_async_copy(n_in, normed, in_sem),
    ]
    for load in loads:
        load.start()
    first = pack_oth.shape[1] - 2 * HD
    do_copy = pltpu.make_async_copy(pack_oth.at[:, pl.ds(first, 2 * HD)], do_oth, do_sem)
    do_copy.start()
    do_copy.wait()
    for h in range(2):
        for b in range(4):
            rows = slice(b * BLK, (b + 1) * BLK)
            do_ref[h, b] = do_own[h, rows]
            do_ref[h, 4 + b] = do_oth[rows, h * HD : (h + 1) * HD]
    needed = chunks_needed(meta)
    loads[0].wait()

    def prepare(chunk, carry):
        rows = rows_of(chunk)
        keys_t[chunk] = k_ref[rows, :].T
        d_keys[rows, :] = jnp.zeros((CHUNK, HD), F32)
        d_values[rows, :] = jnp.zeros((CHUNK, HD), F32)
        return carry

    lax.fori_loop(0, needed, prepare, 0)
    loads[1].wait()

    def tile(t, carry):
        b0, b1, chunks, limit = tile_facts(meta, t)
        queries = tile_rows(q_ref, b0, b1)
        grads = tile_rows(do_ref, b0, b1)
        inverse = inv_ref[t, 0:1, :]
        grads_t = grads.astype(F32).T
        center = jnp.sum(grads_t * ot_ref[t].astype(F32), axis=0, keepdims=True)
        acc[...] = jnp.zeros_like(acc)

        def step(chunk, inner):
            rows = rows_of(chunk)
            scores = dot_nt(k_ref[rows, :], queries)
            ratio = jnp.tanh(scores * (1.0 / CAP))
            probs = jnp.exp(CAP * ratio) * inverse
            at = chunk * CHUNK + lax.broadcasted_iota(jnp.int32, (CHUNK, 4 * BLK), 0)
            probs = jnp.where(at <= limit, probs, 0.0)
            d_probs = dot_nt(v_ref[rows, :], grads)
            d_scores = (probs * (d_probs - center) * (1.0 - ratio * ratio)).astype(BF16)
            d_values[rows, :] += dot(probs.astype(BF16), grads)
            d_keys[rows, :] += dot(d_scores, queries)
            acc[...] += dot(keys_t[chunk], d_scores)
            return inner

        lax.fori_loop(0, chunks, step, 0)
        turned = acc[...].T * HD ** (-0.5)
        for i, (block, place) in enumerate(((b0, 80 + 2 * t), (b1, 81 + 2 * t))):
            cosine, sine = block_tables(tables, meta[place])
            for h in range(2):
                part = turned[(2 * h + i) * BLK : (2 * h + i + 1) * BLK]
                first, second = part[:, :HALF], part[:, HALF:]
                dq[block_rows(block), h * HD : h * HD + HALF] = (
                    first * cosine + second * sine
                ).astype(BF16)
                dq[block_rows(block), h * HD + HALF : (h + 1) * HD] = (
                    second * cosine - first * sine
                ).astype(BF16)
        return carry

    lax.fori_loop(0, 4, tile, 0)
    loads[2].wait()
    kv_grad[...] = jnp.zeros_like(kv_grad)

    def finish(chunk, carry):
        rows = rows_of(chunk)
        cosine, sine = chunk_tables(tables, chunk)
        first, second = d_keys[rows, :HALF], d_keys[rows, HALF:]
        d_both[rows, :HALF] = (first * cosine + second * sine).astype(BF16)
        d_both[rows, HALF:HD] = (second * cosine - first * sine).astype(BF16)
        d_both[rows, HD:] = d_values[rows, :].astype(BF16)
        kv_grad[...] += dot_tn(d_both[rows, :], normed[rows, :])
        return carry

    lax.fori_loop(0, needed, finish, 0)

    def clear(chunk, carry):
        d_both[rows_of(chunk), :] = jnp.zeros((CHUNK, 2 * HD), BF16)
        return carry

    lax.fori_loop(needed, 8, clear, 0)
    for n in range(16):
        for b in range(4):
            target = near_ref.at[n] if n < 8 else far_ref.at[n - 8]
            pltpu.make_async_copy(
                d_both.at[block_rows(meta[n * 4 + b]), :], target.at[pl.ds(b * BLK, BLK), :], out_sem
            ).start()

    for b in range(8):
        normed_q[b * BLK : (b + 1) * BLK, :] = normed[block_rows(q_block(meta, b)), :]
    q_next = qkv_next[: q_own.shape[0], :HD]
    partial = dot_nt(dq[:, :HD], q_own[...]) + dot_nt(dq[:, HD:], q_next)
    dn_own[...] = partial[: 4 * BLK]
    dn_give[...] = partial[4 * BLK :].astype(BF16)
    weighed = jnp.sum(kv_grad[...] * kv_w[...].T.astype(F32), axis=0, keepdims=True)
    for h, weight in enumerate((q_own[...], q_next)):
        q_grad = dot_tn(dq[:, h * HD : (h + 1) * HD], normed_q[...])
        weighed = weighed + jnp.sum(q_grad * weight.T.astype(F32), axis=0, keepdims=True)
        terms_ref[h, :HD, :] = q_grad
    gain_rows = jnp.concatenate(
        [weighed / (1.0 + gains[0:1, :]), gain_in[1:8, :], jnp.zeros((8, gains.shape[1]), F32)], axis=0
    )
    yh, c = meta[65], meta[66]
    quarter = HD // 4
    for h in range(2):
        side = yh if h == 0 else 1 - yh
        for kv in range(2):
            mine = pl.ds(pl.multiple_of(kv * HD + (2 * side + c) * quarter, quarter), quarter)
            theirs = pl.ds(pl.multiple_of(kv * HD + (2 * side + 1 - c) * quarter, quarter), quarter)
            terms_ref[h, HD + kv * quarter : HD + (kv + 1) * quarter, :] = kv_grad[mine, :]
            at = h * 2 * quarter + kv * quarter
            give_ref[at : at + quarter, :] = kv_grad[theirs, :].astype(BF16)
        terms_ref[h, HD + 2 * quarter : HD + 2 * quarter + 16, :] = gain_rows
        terms_ref[h, HD + 2 * quarter + 16 :, :] = jnp.zeros((2 * quarter - 16, gains.shape[1]), F32)
    give_ref[4 * quarter :, :] = gain_rows.astype(BF16)
    pltpu.make_async_copy(d_both, d_both, out_sem).wait()


def attend(meta, weights, gains, tables, pieces, after):
    width = pieces[0].shape[1]
    return pl.pallas_call(
        functools.partial(attend_kernel, len(after)),
        out_shape=(
            shape((2, 8, BLK, HD), BF16),
            shape((2, 4 * BLK, HD), BF16),
            shape((2, 4 * BLK, HD), BF16),
            shape((4, HD, 4 * BLK), BF16),
            shape((4, 8, 4 * BLK), F32),
            shape((width, 2 * HD), BF16),
            shape((SLOTS, width), BF16),
            shape((SLOTS, HD), BF16),
            shape((SLOTS, HD), BF16),
        ),
        in_specs=[SMEM_SPEC] + [VMEM_SPEC] * 6 + [ANY_SPEC] * (10 + len(after)),
        out_specs=(VMEM_SPEC,) * 6 + (HBM_SPEC,) * 3,
        scratch_shapes=[
            pltpu.VMEM((SLOTS, width), BF16),
            pltpu.VMEM((8 * BLK, width), BF16),
            pltpu.VMEM((SLOTS, HD), BF16),
            pltpu.VMEM((SLOTS, HD), BF16),
            pltpu.VMEM((SLOTS // CHUNK, HD, CHUNK), BF16),
            pltpu.VMEM((HD, 4 * BLK), F32),
            pltpu.VMEM((8, 4 * BLK), F32),
            DMA,
            DMA,
            DMA,
            DMA,
        ],
        compiler_params=params(VMEM),
        cost_estimate=cost(20, 20),
        name="attend",
    )(meta, *weights, gains, tables, *pieces, *after)


def attend_back(meta, queries, d_own, d_oth, mixed_t, inverse, keys, values, weights, gains, gain_in, tables, normed, feed_terms):
    width = normed.shape[1]
    rows = 4 * BLK
    return pl.pallas_call(
        attend_back_kernel,
        out_shape=(
            shape((2, 2 * HD, width), F32),
            shape((HD + 16, width), BF16),
            shape((rows, width), F32),
            shape((rows, width), BF16),
            shape((8, rows, 2 * HD), BF16),
            shape((8, rows, 2 * HD), BF16),
        ),
        in_specs=[SMEM_SPEC] + [VMEM_SPEC] * 2 + [ANY_SPEC] + [VMEM_SPEC] * 8 + [HBM_SPEC] * 3 + [ANY_SPEC],
        out_specs=(VMEM_SPEC,) * 4 + (ANY_SPEC,) * 2,
        scratch_shapes=[
            pltpu.VMEM((2, 8, BLK, HD), BF16),
            pltpu.VMEM((rows, 2 * HD), BF16),
            pltpu.VMEM((SLOTS, width), BF16),
            pltpu.VMEM((SLOTS, HD), BF16),
            pltpu.VMEM((SLOTS, HD), BF16),
            pltpu.VMEM((2 * rows, width), BF16),
            pltpu.VMEM((2 * rows, 2 * HD), BF16),
            pltpu.VMEM((2 * HD, width), F32),
            pltpu.VMEM((SLOTS // CHUNK, HD, CHUNK), BF16),
            pltpu.VMEM((SLOTS, HD), F32),
            pltpu.VMEM((SLOTS, HD), F32),
            pltpu.VMEM((SLOTS, 2 * HD), BF16),
            pltpu.VMEM((HD, 4 * BLK), F32),
            DMA,
            DMA,
            DMA,
            DMA,
            DMA,
        ],
        compiler_params=params(VMEM),
        cost_estimate=cost(40, 30),
        name="attend_back",
    )(meta, queries, d_own, d_oth, mixed_t, inverse, *weights, gains, gain_in, tables, keys, values, normed, feed_terms)


GELU_A, GELU_B = 0.7978845608028654, 0.044715


def feed_kernel(meta, gains, mix_own, mix_oth, tok0, tok1, cot0, cot1, *refs):
    weights = refs[:8]
    result0, result1, d_middle_ref, keep_mix, pack, keep, gain_ref = refs[8:15]
    wdo, wgu, zs, sems = refs[15:]
    rows, width = 2 * tok0.shape[0], tok0.shape[1]
    hid = wgu.shape[2] // 2
    copies = [pltpu.make_async_copy(weights[s], wdo.at[s], sems.at[s]) for s in range(4)]
    copies += [pltpu.make_async_copy(weights[4 + s], wgu.at[s], sems.at[4 + s]) for s in range(4)]
    for copy in copies:
        copy.start()
    gain_b, gain_c, gain_d = gains[1:2, :], gains[2:3, :], gains[3:4, :]
    valid = []
    for b in range(4):
        inner = lax.broadcasted_iota(jnp.int32, (BLK, 1), 0)
        valid.append(meta[b] * BLK + inner < meta[64])
    valid = jnp.concatenate([v.astype(F32) for v in valid], axis=0) > 0.5
    start = jnp.concatenate([tok0[...].astype(F32), tok1[...].astype(F32)], axis=0)
    branch = jnp.zeros((rows, width), F32)
    for s in range(4):
        copies[s].wait()
        mixed = mix_own[s] if s < 2 else mix_oth[s - 2]
        branch = branch + dot(mixed, wdo[s, hid:, :])
    middle = start + branch * inverse_rms(branch) * (1.0 + gain_b)
    second = (middle * inverse_rms(middle) * (1.0 + gain_c)).astype(BF16)
    pack[:, :width] = second
    output = jnp.zeros((rows, width), F32)
    at = 3 * width
    for s in range(4):
        copies[4 + s].wait()
        both = dot(second, wgu[s])
        zs[s] = both
        gate, up = both[:, :hid], both[:, hid:]
        bent = jnp.tanh(GELU_A * (gate + GELU_B * gate * gate * gate))
        hidden = (0.5 * gate * (1.0 + bent) * up).astype(BF16)
        if s < 2:
            keep[:, s * hid : (s + 1) * hid] = hidden
        else:
            pack[:, at + (s - 2) * hid : at + (s - 1) * hid] = hidden
        output = output + dot(hidden, wdo[s, :hid, :])
    result = jnp.where(
        valid, middle + output * inverse_rms(output) * (1.0 + gain_d), 0.0
    ).astype(BF16)
    result0[...] = result[: rows // 2]
    result1[...] = result[rows // 2 :]
    cot = jnp.concatenate([cot0[...].astype(F32), cot1[...].astype(F32)], axis=0)
    seed = jnp.where(valid, cot, 0.0)
    d_output, d_gain_d = norm_back(output, gain_d, seed)
    d_output = d_output.astype(BF16)
    pack[:, width : 2 * width] = d_output
    d_second = jnp.zeros((rows, width), F32)
    for s in range(4):
        d_hidden = dot_nt(d_output, wdo[s, :hid, :])
        gate, up = zs[s, :, :hid], zs[s, :, hid:]
        square = gate * gate
        bent = jnp.tanh(GELU_A * gate * (1.0 + GELU_B * square))
        slope = 0.5 * (1.0 + bent) + (0.5 * GELU_A) * gate * (1.0 - bent * bent) * (
            1.0 + 3.0 * GELU_B * square
        )
        d_gate = (d_hidden * up * slope).astype(BF16)
        d_up = (d_hidden * (0.5 * gate * (1.0 + bent))).astype(BF16)
        if s < 2:
            where = 2 * hid + s * 2 * hid
            keep[:, where : where + hid] = d_gate
            keep[:, where + hid : where + 2 * hid] = d_up
        else:
            where = at + 2 * hid + (s - 2) * 2 * hid
            pack[:, where : where + hid] = d_gate
            pack[:, where + hid : where + 2 * hid] = d_up
        d_second = d_second + dot_nt(d_gate, wgu[s, :, :hid]) + dot_nt(d_up, wgu[s, :, hid:])
    d_mid, d_gain_c = norm_back(middle, gain_c, d_second)
    d_middle = seed + d_mid
    d_middle_ref[...] = d_middle
    d_branch, d_gain_b = norm_back(branch, gain_b, d_middle)
    d_branch = d_branch.astype(BF16)
    pack[:, 2 * width : 3 * width] = d_branch
    for s in range(4):
        d_mixed = dot_nt(d_branch, wdo[s, hid:, :]).astype(BF16)
        if s < 2:
            keep_mix[s] = d_mixed
        else:
            pack[:, at + 6 * hid + (s - 2) * HD : at + 6 * hid + (s - 1) * HD] = d_mixed
    zero = jnp.zeros((1, width), F32)
    gain_ref[...] = jnp.concatenate(
        [zero, d_gain_b[None], d_gain_c[None], d_gain_d[None], zero, zero, zero, zero], axis=0
    )


def feed(meta, gains, mix_own, mix_oth, tok, cot, do_weights, gu_weights):
    rows, width = 2 * tok[0].shape[0], tok[0].shape[1]
    hid = gu_weights[0].shape[1] // 2
    do_rows = do_weights[0].shape[0]
    return pl.pallas_call(
        feed_kernel,
        out_shape=(
            shape((rows // 2, width), BF16),
            shape((rows // 2, width), BF16),
            shape((rows, width), F32),
            shape((2, rows, HD), BF16),
            shape((rows, 3 * width + 6 * hid + 2 * HD), BF16),
            shape((rows, 6 * hid), BF16),
            shape((8, width), F32),
        ),
        in_specs=[SMEM_SPEC] + [VMEM_SPEC] * 7 + [ANY_SPEC] * 8,
        out_specs=(VMEM_SPEC,) * 7,
        scratch_shapes=[
            pltpu.VMEM((4, do_rows, width), BF16),
            pltpu.VMEM((4, width, 2 * hid), BF16),
            pltpu.VMEM((4, rows, 2 * hid), F32),
            pltpu.SemaphoreType.DMA((8,)),
        ],
        compiler_params=params(VMEM),
        cost_estimate=cost(5, 16),
        name="feed",
    )(meta, gains, mix_own, mix_oth, *tok, *cot, *do_weights, *gu_weights)


FEED_A, FEED_B, QKV = 64, 48, 32
FEED = FEED_A + FEED_B


def cut_shares(source, x, size, a_rows, a_outs, b_out):
    for z in range(4):
        for s in range(2):
            for r in range(4):
                n = z * 4 + lax.rem(x + r, 4)
                rows = pl.ds(pl.multiple_of(n * size, 16), a_rows)
                a_outs[r][z, s] = source[s, rows, :].astype(BF16)
                first = (z * 4 + r) * size
                b_out[z, r, s] = source[s, first + a_rows : first + size, :].astype(BF16)


def feed_grads_kernel(meta, own, oth, keep, mix_own, mix_oth, a0, a1, a2, a3, b_out, whole):
    hid = keep.shape[1] // 6
    width = whole.shape[2]
    at = 3 * width
    for s in range(2):
        for part in range(2):
            mine = 2 * hid + (2 * s + part) * hid
            theirs = at + 2 * hid + (2 * s + part) * hid
            value = dot_tn(keep[:, mine : mine + hid], own[:, :width])
            value = value + dot_tn(oth[:, theirs : theirs + hid], oth[:, :width])
            whole[s, part * hid : (part + 1) * hid, :] = value.astype(BF16)
        value = dot_tn(keep[:, s * hid : (s + 1) * hid], own[:, width : 2 * width])
        value = value + dot_tn(oth[:, at + s * hid : at + (s + 1) * hid], oth[:, width : 2 * width])
        whole[s, 2 * hid : 3 * hid, :] = value.astype(BF16)
        value = dot_tn(mix_own[s], own[:, 2 * width : 3 * width])
        value = value + dot_tn(mix_oth[s], oth[:, 2 * width : 3 * width])
        whole[s, 3 * hid :, :] = value.astype(BF16)
    cut_shares(whole, meta[69], FEED, FEED_A, (a0, a1, a2, a3), b_out)


def feed_sum_kernel(meta, a0, a1, a2, a3, b_in, *outs):
    a_outs, b_outs = outs[:4], outs[4:]
    x, z = meta[69], meta[70]
    for s in range(2):
        for r in range(4):
            to = lax.rem(z + r, 4)
            total = a0[to, s].astype(F32) + a1[to, s].astype(F32)
            total = total + a2[to, s].astype(F32) + a3[to, s].astype(F32)
            a_outs[r][s] = total.astype(BF16)
            to = lax.rem(x + r, 4)
            total = b_in[0, to, s].astype(F32) + b_in[1, to, s].astype(F32)
            total = total + b_in[2, to, s].astype(F32) + b_in[3, to, s].astype(F32)
            b_outs[r][s] = total.astype(BF16)


def grad_join_kernel(a0, a1, a2, a3, b0, b1, b2, b3, qkv, *outs):
    for s, out in enumerate(outs):
        total = a0[s].astype(F32) + a1[s].astype(F32) + a2[s].astype(F32) + a3[s].astype(F32)
        out[:FEED_A] = total.astype(BF16)
        total = b0[s].astype(F32) + b1[s].astype(F32) + b2[s].astype(F32) + b3[s].astype(F32)
        out[FEED_A:FEED] = total.astype(BF16)
        total = qkv[0, s].astype(F32)
        for n in range(1, 16):
            total = total + qkv[n, s].astype(F32)
        out[FEED:] = total.astype(BF16)


def grad_total_kernel(a, b, c, d, out):
    total = a[...].astype(F32) + b[...].astype(F32) + c[...].astype(F32) + d[...].astype(F32)
    out[...] = jnp.broadcast_to(total.astype(BF16)[None], out.shape)


def grad_out_kernel(got, gate, up, down, out, q_out, k_out, v_out, gain_out):
    hid = gate.shape[1]
    whole = jnp.concatenate([got[n, :FEED].astype(F32) for n in range(16)], axis=0)
    gate[...] = whole[:hid].T
    up[...] = whole[hid : 2 * hid].T
    down[...] = whole[2 * hid : 3 * hid]
    out[...] = whole[3 * hid :]
    small = jnp.concatenate([got[n, FEED:].astype(F32) for n in range(16)], axis=0)
    quarter = HD // 4
    q_out[...] = small[:HD].T
    k_out[...] = small[HD : HD + quarter]
    v_out[...] = small[HD + quarter : HD + 2 * quarter]
    gain_out[...] = small[HD + 2 * quarter : HD + 2 * quarter + 8]


def sum_a_kernel(near, far, g0, g1, k0, k1):
    gives, keeps = (g0, g1), (k0, k1)
    for p, (first, last, (a, b, d)) in enumerate(BACK_PARTS):
        size = last - first
        for i, move in enumerate((0, a, b, a | b)):
            rows = pl.ds(i * size, size)
            for out, at in ((keeps[p], move), (gives[p], move | d)):
                both = near[at, first:last].astype(F32) + far[at, first:last].astype(F32)
                out[rows, :] = both.astype(out.dtype)


def qkv_shares_kernel(terms, got, shares):
    half = HD // 2
    for h in range(2):
        for n in range(16):
            at = n * QKV
            value = terms[h, at : at + QKV]
            if HD <= at < HD + half:
                from_row = h * half + at - HD
                value = value + got[from_row : from_row + QKV].astype(F32)
            if at == HD + half:
                rest = jnp.zeros((QKV - 16, terms.shape[2]), F32)
                value = value + jnp.concatenate([got[HD:].astype(F32), rest], axis=0)
            shares[n, h] = value.astype(BF16)


def halves(keeps, gots, outs):
    for p in range(2):
        rows = keeps[p].shape[0] // 2
        outs[p][...] = (keeps[p][rows:] + gots[p][rows:].astype(F32)).astype(BF16)
        outs[2 + p][...] = keeps[p][:rows] + gots[p][:rows].astype(F32)


def sum_b_kernel(k0, k1, g0, g1, *outs):
    halves((k0, k1), (g0, g1), outs)


def sum_d_kernel(k0, k1, g0, g1, dn, dn_got, tok0, tok1, d_middle, kv_w, gains, t0, t1):
    d_kv = [k[...] + g[...].astype(F32) for k, g in ((k0, g0), (k1, g1))]
    d_kv = jnp.concatenate(d_kv, axis=0).astype(BF16)
    d_normed = dn[...] + dn_got[...].astype(F32) + dot_nt(d_kv, kv_w[...])
    start = jnp.concatenate([tok0[...].astype(F32), tok1[...].astype(F32)], axis=0)
    d_start, _ = norm_back(start, gains[0:1, :], d_normed)
    grads = (d_middle[...] + d_start).astype(BF16)
    half = t0.shape[0]
    t0[...] = grads[:half]
    t1[...] = grads[half:]


def on_device(
    tokens,
    cotangent,
    lengths,
    block_order,
    query_weight,
    key_weight,
    value_weight,
    out_weight,
    gate_weight,
    up_weight,
    down_weight,
    gain_attn_in,
    gain_attn_out,
    gain_ffn_in,
    gain_ffn_out,
):
    ctx, fsdp = lax.axis_index("ctx"), lax.axis_index("fsdp")
    yl, z, x = ctx // 16, (ctx // 4) % 4, ctx % 4
    yh, c = fsdp // 2, fsdp % 2
    zh, zl, xh, xl = z // 2, z % 2, x // 2, x % 2
    low_y, low_c, low_x = yh == 0, c == 0, xh == 0
    own_rows = 4 * BLK
    width = tokens.shape[-1]

    def rows_to(array):
        return (
            send(jnp.where(low_x, array[0, 0], array[0, 1]), regroup(0)),
            send(jnp.where(low_x, array[0, 1], array[0, 0]), regroup(1)),
        )

    def rows_back(first, second):
        first, second = send(first, regroup(0)), send(second, regroup(1))
        return jnp.stack([jnp.where(low_x, first, second), jnp.where(low_x, second, first)])[None]

    tok0, tok1 = rows_to(tokens)
    part_shapes = [shape((size, width), BF16) for size in sizes()]
    spot = jnp.stack([yh, c, zh, zl, xh, xl, yl, fsdp]).astype(jnp.int32)
    part_shapes = [shape((size, width), BF16) for size in sizes()]
    heads = HD
    quarter = key_weight.shape[1]
    hidden_cols = gate_weight.shape[1]
    share = gain_attn_in.shape[0]
    length_parts = jnp.concatenate([lengths // 64, lengths % 64], axis=0).astype(BF16)
    gains = jnp.stack([gain_attn_in, gain_attn_out, gain_ffn_in, gain_ffn_out])
    gains = jnp.concatenate([gains, jnp.pad(length_parts, ((0, 0), (0, share - 2)))], axis=0)
    (qkv_own,) = step(
        pack_qkv_kernel,
        [shape((width + 16, heads + 2 * quarter), BF16)],
        (query_weight, key_weight.T, value_weight.T, gains),
        mbytes=6,
        name="pack_qkv",
    )
    qkv_next = send(qkv_own, to_next)
    parts = step(cut_kernel, part_shapes, (tok0, tok1), after=(qkv_own,), mbytes=6, name="cut")

    def cube_send(arrays, stage):
        return [send(array, to_cube(order[stage])) for array, (first, last, order) in zip(arrays, PARTS)]

    got = cube_send(parts, 0)

    (do_own,) = step(
        pack_rows_kernel,
        [shape((hidden_cols + heads, width), BF16)],
        (down_weight, out_weight),
        after=(parts[0],),
        name="pack_do",
    )
    do_next = send(do_own, to_next)
    do_swap = send(do_own, to_core)
    pairs = step(
        functools.partial(join_kernel, 3),
        [shape((2 * size, width), BF16) for size in sizes()],
        (*parts, *got),
        after=(do_own,),
        mbytes=6,
        name="join",
    )
    got = cube_send(pairs, 1)

    (kv_pair,) = step(
        kv_pair_kernel,
        [shape((width + 32, 4 * quarter), BF16)],
        (qkv_own, qkv_next),
        meta=spot,
        mbytes=6,
        name="kv_pair",
    )
    kv_other = send(kv_pair, to_core)
    mine, theirs = (
        m[width:, :share].reshape(2, 16, share)[:, :6] for m in (kv_pair, kv_other)
    )
    quarters = jnp.stack(
        [jnp.where(low_c, mine, theirs), jnp.where(low_c, theirs, mine)], axis=1
    )
    all_gains = jnp.transpose(quarters[:, :, :4], (2, 0, 1, 3)).reshape(4, width).astype(F32)
    gain_rows = jnp.concatenate([all_gains, jnp.zeros((4, width), F32)], axis=0)
    lengths_here = jnp.where(low_y, quarters[0, :, 4:, :2], quarters[1, :, 4:, :2])
    lengths_here = jnp.where(zh == 0, lengths_here[0], lengths_here[1]).astype(jnp.int32)
    lengths_here = lengths_here[0] * 64 + lengths_here[1]
    length = jnp.where(low_x, lengths_here[0], lengths_here[1])

    joined = step(
        join_all_kernel,
        [shape((4 * size, width), BF16) for size in sizes()] + [shape((4 * own_rows, width), BF16)],
        (*pairs, *got),
        after=(kv_pair,),
        mbytes=8,
        name="join_all",
    )
    low_parts, low_all = joined[:3], joined[3]
    high_parts = cube_send(low_parts, 2)
    (gu_own,) = step(
        pack_columns_kernel,
        [shape((width, 2 * hidden_cols), BF16)],
        (gate_weight, up_weight),
        after=(do_next, high_parts[0]),
        name="pack_gu",
    )

    stored = []
    for other in range(2):
        for move in range(8):
            dy, dz, dx = move >> 2, (move >> 1) & 1, move & 1
            for turn in range(2):
                place = (yl ^ dy) * 16 + ((c ^ other) * 2 + (zl ^ dz)) * 4
                place = place + (xh ^ turn) * 2 + (xl ^ dx)
                stored += [place * 2, place * 2 + 1]
    stored = jnp.stack(stored)
    slots = jnp.arange(64, dtype=jnp.int32)
    block_at = jnp.sum(
        jnp.where(stored[:, None] == slots[None, :], block_order[None, :], 0), axis=1
    ).astype(jnp.int32)
    q_blocks = jnp.concatenate([block_at[0:4], block_at[32:36]])
    rank = jnp.sum((q_blocks[None, :] < q_blocks[:, None]).astype(jnp.int32), axis=1)
    eight = jnp.arange(8, dtype=jnp.int32)
    chosen = rank[None, :] == eight[:, None]
    order = jnp.sum(jnp.where(chosen, eight[None, :], 0), axis=1).astype(jnp.int32)
    order_block = jnp.sum(jnp.where(chosen, q_blocks[None, :], 0), axis=1).astype(jnp.int32)
    facts = jnp.stack([length, yh, c, zh, xh, x, z, z]).astype(jnp.int32)
    meta = jnp.concatenate([block_at, facts, order, order_block])

    low_all = send(low_all, to_core)
    high_far = [send(part, to_core) for part in high_parts]
    pieces = list(low_parts) + high_parts + [low_all] + high_far
    tables = jnp.asarray(angle_tables())
    gu_next = send(gu_own, to_next)
    do_next_swap = send(do_next, to_core)
    do_weights = [do_own, do_next, do_swap, do_next_swap]
    gu_swap = send(gu_own, to_core)
    half_shape = shape((own_rows // 2, width), BF16)
    cot0, cot1 = step(
        pick_kernel,
        [half_shape, half_shape],
        (cotangent[0],),
        after=(joined[0],),
        meta=spot,
        mbytes=6,
        name="pick_cot",
    )
    cot0, cot1 = send(cot0, regroup(0)), send(cot1, regroup(1))
    queries, mix_own, mix_oth, mixed_t, inverse, kv_weight, sorted_normed, keys, values = attend(
        meta, (query_weight, qkv_next, kv_pair, kv_other), gain_rows, tables, pieces, (do_swap, do_next_swap, gu_swap)
    )

    (gu_next,) = gate((gu_next,), (mix_own, cot0, cot1))
    gu_weights = [gu_own, gu_next, gu_swap, send(gu_next, to_core)]
    result0, result1, d_middle, keep_mix, pack, keep, gain_terms = feed(
        meta, gain_rows, mix_own, send(mix_oth, to_core), (tok0, tok1), (cot0, cot1), do_weights, gu_weights
    )
    pack_oth = send(pack, to_core)
    a_shape = shape((4, 2, FEED_A, width), BF16)
    *feed_a, feed_b = step(
        feed_grads_kernel,
        [a_shape] * 4 + [shape((4, 4, 2, FEED_B, width), BF16)],
        (pack, pack_oth, keep, mix_own, mix_oth),
        meta=meta,
        name="feed_grads",
        scratch=[pltpu.VMEM((2, 3 * hidden_cols + HD, width), BF16)],
    )
    feed_a_got = spread(feed_a[1:], along_x)
    feed_b_got = swap_z(feed_b)

    terms, core_give, dn_own, dn_give, d_near, d_far = attend_back(
        meta,
        queries,
        keep_mix,
        pack_oth,
        mixed_t,
        inverse,
        keys,
        values,
        (query_weight, qkv_next, kv_weight),
        gain_rows,
        gain_terms,
        tables,
        sorted_normed,
        feed_b,
    )
    d_far, core_give, dn_give = gate((d_far, core_give, dn_give), (*feed_a_got, feed_b_got))
    d_far, core_got, dn_got = send(d_far, to_core), send(core_give, to_core), send(dn_give, to_core)

    def part_shape(count, dtype):
        return [shape((count * (last - first), 2 * HD), dtype) for first, last, order in BACK_PARTS]

    def rows_shape(*dims):
        return shape((*dims, width), BF16)

    def cube_return(arrays, stage):
        return [
            send(array, to_cube(order[stage])) for array, (first, last, order) in zip(arrays, BACK_PARTS)
        ]

    feed_outs = step(
        feed_sum_kernel,
        [rows_shape(2, FEED_A)] * 4 + [rows_shape(2, FEED_B)] * 4,
        (feed_a[0], *feed_a_got, feed_b_got),
        after=(core_give,),
        meta=meta,
        name="feed_sum",
    )
    feed_parts = [feed_outs[0], *spread(feed_outs[1:4], along_z), feed_outs[4], *spread(feed_outs[5:8], along_x)]
    outs = step(
        sum_a_kernel,
        part_shape(4, BF16) + part_shape(4, F32),
        (d_near, d_far),
        after=(feed_outs[0],),
        name="sum_a",
    )
    got, keeps = cube_return(outs[:2], 2), outs[2:4]
    (qkv_terms,) = step(
        qkv_shares_kernel,
        [rows_shape(16, 2, QKV)],
        (terms, core_got),
        after=(outs[0], *feed_parts),
        name="qkv_shares",
    )
    qkv_got = swap_plane(qkv_terms)
    outs = step(
        sum_b_kernel,
        part_shape(2, BF16) + part_shape(2, F32),
        (*keeps, *got),
        after=(qkv_terms,),
        name="sum_b",
    )
    got, keeps = cube_return(outs[:2], 1), outs[2:4]
    result0, result1 = gate((result0, result1), (outs[0],))
    result_block = rows_back(result0, result1)
    outs = step(
        sum_b_kernel, part_shape(1, BF16) + part_shape(1, F32), (*keeps, *got), name="sum_c"
    )
    got, keeps = cube_return(outs[:2], 0), outs[2:4]
    mine, theirs = step(
        grad_join_kernel,
        [rows_shape(FEED + QKV)] * 2,
        (*feed_parts, qkv_got),
        after=(outs[0],),
        name="grad_join",
    )
    y_got = [send(mine, to_yl), send(theirs, to_next), send(theirs, to_yh)]
    tok_back0, tok_back1 = step(
        sum_d_kernel,
        [rows_shape(own_rows // 2)] * 2,
        (*keeps, *got, dn_own, dn_got, tok0, tok1, d_middle, kv_weight, gain_rows),
        after=(mine,),
        name="sum_d",
    )
    token_block = rows_back(tok_back0, tok_back1).astype(F32)
    (all_grads,) = step(
        grad_total_kernel,
        [rows_shape(16, FEED + QKV)],
        (mine, *y_got),
        after=(tok_back0, result_block),
        name="grad_total",
    )
    all_grads = swap_plane(all_grads)
    gate_grad, up_grad, down_grad, out_grad, q_grad, k_grad, v_grad, gain_sum = step(
        grad_out_kernel,
        [
            shape((width, hidden_cols), F32),
            shape((width, hidden_cols), F32),
            shape((hidden_cols, width), F32),
            shape((HD, width), F32),
            shape((width, HD), F32),
            shape((quarter, width), F32),
            shape((quarter, width), F32),
            shape((8, width), F32),
        ],
        (all_grads,),
        name="grad_out",
    )
    share_rows = width // 4
    gain_grads = lax.dynamic_slice_in_dim(gain_sum, fsdp * share_rows, share_rows, axis=1)
    return (
        result_block,
        token_block,
        q_grad,
        k_grad.T,
        v_grad.T,
        out_grad,
        gate_grad,
        up_grad,
        down_grad,
        gain_grads[0],
        gain_grads[1],
        gain_grads[2],
        gain_grads[3],
    )


def solution(mesh):
    rows, cols, first = P("fsdp", None, "ctx", None), P(None, "fsdp"), P("fsdp", None)
    weights = (cols, cols, cols, first, cols, cols, first)
    gains = (P("fsdp"),) * 4
    return jax.shard_map(
        on_device,
        mesh=mesh,
        in_specs=(rows, rows, first, P()) + weights + gains,
        out_specs=(rows, rows) + weights + gains,
        check_vma=False,
    )
```

```python
import functools

import jax
import jax.numpy as jnp
import numpy as np
from jax import lax
from jax.experimental import pallas as pl
from jax.experimental.pallas import tpu as pltpu
from jax.sharding import PartitionSpec as P

F32, BF16 = jnp.float32, jnp.bfloat16
CAP = 50.0
CAP_LOG2 = CAP * 1.4426950408889634
EPS = 1e-06
BASE = 1000000.0
HD = 256
HALF = HD // 2
BLK = 64
CHUNK = 512
VMEM = 54
AXES = ("ctx", "fsdp")


def all_places():
    for yl in range(2):
        for z in range(4):
            for x in range(4):
                for yh in range(2):
                    for c in range(2):
                        yield yl, z, x, yh, c


def flat(yl, z, x, yh, c):
    return (((yl * 4 + z) * 4 + x) * 2 + yh) * 2 + c


def send(array, move):
    pairs = [(flat(*p), flat(*move(*p))) for p in all_places()]
    return lax.ppermute(array, AXES, pairs)


def to_core(yl, z, x, yh, c):
    return yl, z, x, yh, 1 - c


def to_next(yl, z, x, yh, c):
    return 1 - yl, z, x, 1 - yh, c


def to_yl(yl, z, x, yh, c):
    return 1 - yl, z, x, yh, c


def to_yh(yl, z, x, yh, c):
    return yl, z, x, 1 - yh, c


def to_zpair(yl, z, x, yh, c):
    return yl, z ^ 1, x, yh, c


def to_xpair(yl, z, x, yh, c):
    return yl, z, x ^ 1, yh, c


def to_zring(yl, z, x, yh, c):
    return yl, (z + (1 if z % 2 else 3)) % 4, x, yh, c


def to_xring(yl, z, x, yh, c):
    return yl, z, (x + (1 if x % 2 else 3)) % 4, yh, c


def regroup(turn):
    def move(yl, z, x, yh, c):
        zh, zl, xh, xl = z // 2, z % 2, x // 2, x % 2
        return yl, c * 2 + zl, (xh ^ turn) * 2 + xl, yh, zh

    return move


def to_cube(step):
    dy, dz, dx = step >> 2, (step >> 1) & 1, step & 1

    def move(yl, z, x, yh, c):
        return yl ^ dy, z ^ dz, x ^ dx, yh, c

    return move


PARTS = ((0, 96, (4, 2, 1)), (96, 176, (2, 1, 4)), (176, 256, (1, 4, 2)))


BACK_PARTS = ((0, 128, (4, 2, 1)), (128, 256, (2, 1, 4)))


def held_by(order):
    a, b, d = order
    low = (0, a, b, a | b)
    return low, tuple(d | step for step in low)


def copy_kernel(array, out):
    out[...] = array[...]


def pack_rows_kernel(first, second, out):
    out[: first.shape[0]] = first[...]
    out[first.shape[0] :] = second[...]


def pack_columns_kernel(first, second, out):
    out[:, : first.shape[1]] = first[...]
    out[:, first.shape[1] :] = second[...]


def pack_qkv_kernel(query, key_t, value_t, gains, out):
    rows, width = query.shape[0], gains.shape[1]
    out[:rows, :HD] = query[...]
    out[:rows, HD:] = jnp.concatenate([key_t[...], value_t[...]], axis=0).T
    out[rows:, :] = jnp.zeros((out.shape[0] - rows, out.shape[1]), BF16)
    out[rows : rows + gains.shape[0], :width] = gains[...]


def kv_pair_kernel(spot, own, after, out):
    low = spot[0] == 0
    half = HD // 2
    rows = own.shape[0] - 16
    mine, theirs = own[:rows, HD:], after[:rows, HD:]
    out[:rows, :half] = jnp.where(low, mine, theirs)
    out[:rows, half:] = jnp.where(low, theirs, mine)
    mine, theirs = own[rows:, :HD], after[rows:, :HD]
    out[rows : rows + 16, :] = jnp.where(low, mine, theirs)
    out[rows + 16 :, :] = jnp.where(low, theirs, mine)


def pick_kernel(spot, array, first, second):
    low = spot[4] == 0
    first[...] = jnp.where(low, array[0], array[1])
    second[...] = jnp.where(low, array[1], array[0])


def sizes():
    return [last - first for first, last, order in PARTS]


def cut_kernel(r0, r1, *outs):
    half = r0.shape[0]
    for (first, last, order), out in zip(PARTS, outs):
        if first < half:
            out[: min(last, half) - first] = r0[first : min(last, half)]
        if last > half:
            out[max(first, half) - first :] = r1[max(first, half) - half : last - half]


def join_kernel(count, *refs):
    ins, outs = refs[: 2 * count], refs[-count:]
    for p in range(count):
        rows = ins[p].shape[0]
        outs[p][:rows] = ins[p][...]
        outs[p][rows:] = ins[count + p][...]


def join_all_kernel(*refs):
    ins, outs = refs[:6], refs[-4:]
    at = 0
    for p in range(3):
        rows = ins[p].shape[0]
        outs[p][:rows] = ins[p][...]
        outs[p][rows:] = ins[3 + p][...]
        outs[3][at : at + rows] = ins[p][...]
        outs[3][at + rows : at + 2 * rows] = ins[3 + p][...]
        at += 2 * rows


PLANE = [[yl * 16 + i for i in range(16)] for yl in range(2)]


def swap_plane(array):
    return lax.all_to_all(
        array, "ctx", split_axis=0, concat_axis=0, axis_index_groups=PLANE, tiled=True
    )


def along_x(shift):
    def move(yl, z, x, yh, c):
        return yl, z, (x + shift) % 4, yh, c

    return move


def along_z(shift):
    def move(yl, z, x, yh, c):
        return yl, (z + shift) % 4, x, yh, c

    return move


def spread(arrays, along):
    return [send(array, along(r + 1)) for r, array in enumerate(arrays)]


ROWS = [[yl * 16 + z * 4 + x for x in range(4)] for yl in range(2) for z in range(4)]
COLUMNS = [[yl * 16 + z * 4 + x for z in range(4)] for yl in range(2) for x in range(4)]


def swap_z(array):
    return lax.all_to_all(
        array, "ctx", split_axis=0, concat_axis=0, axis_index_groups=COLUMNS, tiled=True
    )


def inverse_rms(values):
    return lax.rsqrt(jnp.mean(values * values, axis=-1, keepdims=True) + EPS)


def norm_back(values, gain, grads):
    scale = inverse_rms(values)
    hat = values * scale
    scaled = grads * (1.0 + gain)
    inner = jnp.mean(scaled * hat, axis=-1, keepdims=True)
    return scale * (scaled - hat * inner), jnp.sum(grads * hat, axis=0)


def dot(left, right):
    return jnp.dot(left, right, preferred_element_type=F32)


def dot_nt(left, right):
    return lax.dot_general(left, right, (((1,), (1,)), ((), ())), preferred_element_type=F32)


def dot_tn(left, right):
    return lax.dot_general(left, right, (((0,), (0,)), ((), ())), preferred_element_type=F32)


def angle_tables():
    freqs = BASE ** (-(np.arange(HALF, dtype=np.float32) * 2.0 / HD)).astype(np.float32)
    coarse = (np.arange(64, dtype=np.float64) * 64)[:, None] * freqs[None, :].astype(np.float64)
    fine = np.arange(BLK, dtype=np.float64)[:, None] * freqs[None, :].astype(np.float64)
    tables = [np.cos(coarse), np.sin(coarse), np.cos(fine), np.sin(fine)]
    return np.stack(tables).astype(np.float32)


SMEM_SPEC = pl.BlockSpec(memory_space=pltpu.SMEM)
VMEM_SPEC = pl.BlockSpec(memory_space=pltpu.VMEM)
ANY_SPEC = pl.BlockSpec(memory_space=pl.ANY)
HBM_SPEC = pl.BlockSpec(memory_space=pltpu.HBM)
DMA = pltpu.SemaphoreType.DMA
SLOTS = 4096


def shape(dims, dtype):
    return jax.ShapeDtypeStruct(dims, dtype)


def cost(gflops, mbytes):
    return pl.CostEstimate(
        flops=int(gflops * 10**9), bytes_accessed=int(mbytes * 10**6), transcendentals=0
    )


def params(mbytes):
    return pltpu.CompilerParams(vmem_limit_bytes=mbytes * 1024 * 1024)


def step(kernel, outs, arrays, after=(), meta=None, mbytes=VMEM, name=None, scratch=()):
    scalars = 0 if meta is None else 1
    used = scalars + len(arrays)

    def body(*refs):
        kernel(*refs[:used], *refs[used + len(after) :])

    return pl.pallas_call(
        body,
        out_shape=tuple(outs),
        in_specs=[SMEM_SPEC] * scalars + [VMEM_SPEC] * len(arrays) + [ANY_SPEC] * len(after),
        out_specs=(VMEM_SPEC,) * len(outs),
        scratch_shapes=list(scratch),
        compiler_params=params(mbytes),
        cost_estimate=cost(0.1, 4),
        name=name,
    )(*(() if meta is None else (meta,)), *arrays, *after)


def gate_kernel(*refs):
    pass


def gate(arrays, after):
    return pl.pallas_call(
        gate_kernel,
        out_shape=tuple(shape(a.shape, a.dtype) for a in arrays),
        in_specs=[ANY_SPEC] * (len(arrays) + len(after)),
        out_specs=(ANY_SPEC,) * len(arrays),
        input_output_aliases={i: i for i in range(len(arrays))},
        name="gate",
    )(*arrays, *after)


def chunk_tables(tables, chunk):
    rows = pl.ds(pl.multiple_of(chunk * 8, 8), 8)
    ca = tables[0, rows, :][:, None, :]
    sa = tables[1, rows, :][:, None, :]
    cb = tables[2][None]
    sb = tables[3][None]
    cosine = (ca * cb - sa * sb).reshape(CHUNK, HALF)
    sine = (sa * cb + ca * sb).reshape(CHUNK, HALF)
    return cosine, sine


def block_tables(tables, block):
    ca, sa = tables[0, pl.ds(block, 1), :], tables[1, pl.ds(block, 1), :]
    cb, sb = tables[2], tables[3]
    return ca * cb - sa * sb, sa * cb + ca * sb


def tile_facts(meta, t):
    b0, b1 = meta[72 + 2 * t], meta[73 + 2 * t]
    p0, p1 = meta[80 + 2 * t], meta[81 + 2 * t]
    length = meta[64]
    last = jnp.minimum(p1 * BLK + BLK, length)
    chunks = jnp.where(p0 * BLK < length, (last + CHUNK - 1) // CHUNK, 0)
    lane = lax.broadcasted_iota(jnp.int32, (1, 4 * BLK), 1)
    second = (lane // BLK) % 2 == 1
    limit = jnp.where(second, p1, p0) * BLK + lane % BLK
    return b0, b1, chunks, jnp.minimum(limit, length - 1)


def whole_chunks(meta, t):
    return jnp.minimum(meta[80 + 2 * t] * BLK + 1, meta[64]) // CHUNK


def over_chunks(step, whole, chunks):
    def plain(chunk, carry):
        step(chunk, False)
        return carry

    def masked(chunk, carry):
        step(chunk, True)
        return carry

    first = jnp.minimum(whole, chunks)
    lax.fori_loop(0, first, plain, 0)
    lax.fori_loop(first, chunks, masked, 0)


def chunks_needed(meta):
    most = jnp.int32(0)
    for t in range(4):
        most = jnp.maximum(most, tile_facts(meta, t)[2])
    return most


def q_block(meta, b):
    return meta[b] if b < 4 else meta[28 + b]


def rows_of(chunk):
    return pl.ds(pl.multiple_of(chunk * CHUNK, CHUNK), CHUNK)


def block_rows(block):
    return pl.ds(pl.multiple_of(block * BLK, BLK), BLK)


def tile_rows(ref, b0, b1):
    return jnp.concatenate([ref[0, b0], ref[0, b1], ref[1, b0], ref[1, b1]], axis=0)


def put_tile(own, oth, b0, b1, tile):
    for block, rows in ((b0, 0), (b1, BLK)):
        for ref, base in ((own, 0), (oth, 4)):

            @pl.when((block >= base) & (block < base + 4))
            def _():
                to = pl.ds(pl.multiple_of((block - base) * BLK, BLK), BLK)
                ref[0, to, :] = tile[rows : rows + BLK]
                ref[1, to, :] = tile[2 * BLK + rows : 3 * BLK + rows]


def attend_kernel(after, meta, q_own, qkv_next, kv_mine, kv_theirs, gains, tables, *refs):
    q_ref, own_ref, oth_ref, ot_ref, inv_ref, w_ref, n_out, k_out, v_out = refs[10 + after : 19 + after]
    normed, normed_q, keys, values, values_t, acc, total, in_sem, n_sem, k_sem, v_sem = refs[19 + after :]
    for core in range(2):
        for p, (first, last, order) in enumerate(PARTS):
            size = last - first
            for half, steps in enumerate(held_by(order)):
                source, base = refs[half * 3 + p], 0
                if core == 1:
                    source = refs[6] if half == 0 else refs[7 + p]
                    base = 4 * first if half == 0 else 0
                for i, step in enumerate(steps):
                    row = first
                    while row < last:
                        block, inner = row // BLK, row % BLK
                        count = min(last - row, BLK - inner)
                        to = pl.multiple_of(meta[(core * 8 + step) * 4 + block] * BLK + inner, 16)
                        pltpu.make_async_copy(
                            source.at[pl.ds(base + i * size + row - first, count), :],
                            normed.at[pl.ds(to, count), :],
                            in_sem,
                        ).start()
                        row += count
    low = meta[66] == 0
    rows = w_ref.shape[0]
    first_core = jnp.where(low, kv_mine[:rows], kv_theirs[:rows])
    second_core = jnp.where(low, kv_theirs[:rows], kv_mine[:rows])
    quarter = HD // 4
    for kv in range(2):
        for side in range(2):
            at = side * 2 * quarter + kv * quarter
            to = kv * HD + side * 2 * quarter
            w_ref[:, to : to + 2 * quarter] = jnp.concatenate(
                [first_core[:, at : at + quarter], second_core[:, at : at + quarter]], axis=1
            )
    pltpu.make_async_copy(normed, normed, in_sem).wait()

    def prepare(chunk, carry):
        rows = rows_of(chunk)
        start = normed[rows, :].astype(F32)
        low_rows = (start * inverse_rms(start) * (1.0 + gains[0:1, :])).astype(BF16)
        normed[rows, :] = low_rows
        both = dot(low_rows, w_ref[...])
        cosine, sine = chunk_tables(tables, chunk)
        first, second = both[:, :HALF], both[:, HALF:HD]
        keys[rows, :HALF] = (first * cosine - second * sine).astype(BF16)
        keys[rows, HALF:] = (second * cosine + first * sine).astype(BF16)
        low = both[:, HD:].astype(BF16)
        values[rows, :] = low
        values_t[chunk] = low.T
        return carry

    lax.fori_loop(0, chunks_needed(meta), prepare, 0)
    copies = [
        pltpu.make_async_copy(normed, n_out, n_sem),
        pltpu.make_async_copy(keys, k_out, k_sem),
        pltpu.make_async_copy(values, v_out, v_sem),
    ]
    for copy in copies:
        copy.start()
    for b in range(8):
        normed_q[b * BLK : (b + 1) * BLK, :] = normed[block_rows(q_block(meta, b)), :]
    for h, weight in enumerate((q_own[...], qkv_next[: q_own.shape[0], :HD])):
        pre = dot(normed_q[...], weight) * HD ** (-0.5)
        for b in range(8):
            cosine, sine = block_tables(tables, q_block(meta, b))
            first = pre[b * BLK : (b + 1) * BLK, :HALF]
            second = pre[b * BLK : (b + 1) * BLK, HALF:]
            q_ref[h, b, :, :HALF] = (first * cosine - second * sine).astype(BF16)
            q_ref[h, b, :, HALF:] = (second * cosine + first * sine).astype(BF16)

    def tile(t, carry):
        b0, b1, chunks, limit = tile_facts(meta, t)
        queries = tile_rows(q_ref, b0, b1)
        acc[...] = jnp.zeros_like(acc)
        total[...] = jnp.zeros_like(total)

        def step(chunk, masked):
            scores = dot_nt(keys[rows_of(chunk), :], queries)
            grown = jnp.exp2(CAP_LOG2 * jnp.tanh(scores * (1.0 / CAP)))
            if masked:
                at = lax.broadcasted_iota(jnp.int32, (CHUNK, 4 * BLK), 0)
                grown = jnp.where(at <= limit - chunk * CHUNK, grown, 0.0)
            total[...] += jnp.sum(grown.reshape(CHUNK // 8, 8, 4 * BLK), axis=0)
            acc[...] += dot(values_t[chunk], grown.astype(BF16))

        over_chunks(step, whole_chunks(meta, t), chunks)
        whole = jnp.sum(total[...], axis=0, keepdims=True)
        inverse = jnp.where(whole > 0.0, 1.0 / jnp.where(whole > 0.0, whole, 1.0), 0.0)
        mixed = acc[...] * inverse
        shift = -jnp.log2(jnp.where(whole > 0.0, whole, 1.0))
        inv_ref[t] = jnp.broadcast_to(shift, (8, 4 * BLK))
        ot_ref[t] = mixed.astype(BF16)
        put_tile(own_ref, oth_ref, b0, b1, mixed.T.astype(BF16))
        return carry

    lax.fori_loop(0, 4, tile, 0)
    for copy in copies:
        copy.wait()


def attend_back_kernel(
    meta, q_ref, do_own, pack_oth, ot_ref, inv_ref, q_own, qkv_next, tables, k_in, v_in, feed_terms,
    dq_ref, both_ref, dn_own, dn_give, near_ref, far_ref, *refs
):
    do_ref, do_oth, k_ref, v_ref, keys_t, d_keys, d_values, d_both, acc, do_sem, k_sem, v_sem, both_sem, out_sem = refs
    loads = [
        pltpu.make_async_copy(k_in, k_ref, k_sem),
        pltpu.make_async_copy(v_in, v_ref, v_sem),
    ]
    for load in loads:
        load.start()
    first = pack_oth.shape[1] - 2 * HD
    do_copy = pltpu.make_async_copy(pack_oth.at[:, pl.ds(first, 2 * HD)], do_oth, do_sem)
    do_copy.start()
    do_copy.wait()
    for h in range(2):
        for b in range(4):
            rows = slice(b * BLK, (b + 1) * BLK)
            do_ref[h, b] = do_own[h, rows]
            do_ref[h, 4 + b] = do_oth[rows, h * HD : (h + 1) * HD]
    needed = chunks_needed(meta)
    loads[0].wait()

    def prepare(chunk, carry):
        rows = rows_of(chunk)
        keys_t[chunk] = k_ref[rows, :].T
        d_keys[rows, :] = jnp.zeros((CHUNK, HD), F32)
        d_values[rows, :] = jnp.zeros((CHUNK, HD), F32)
        return carry

    lax.fori_loop(0, needed, prepare, 0)
    loads[1].wait()

    def tile(t, carry):
        b0, b1, chunks, limit = tile_facts(meta, t)
        queries = tile_rows(q_ref, b0, b1)
        grads = tile_rows(do_ref, b0, b1)
        shift = inv_ref[t, 0:1, :]
        grads_t = grads.astype(F32).T
        center = jnp.sum(grads_t * ot_ref[t].astype(F32), axis=0, keepdims=True)
        acc[...] = jnp.zeros_like(acc)

        def step(chunk, masked):
            rows = rows_of(chunk)
            scores = dot_nt(k_ref[rows, :], queries)
            ratio = jnp.tanh(scores * (1.0 / CAP))
            probs = jnp.exp2(CAP_LOG2 * ratio + shift)
            if masked:
                at = lax.broadcasted_iota(jnp.int32, (CHUNK, 4 * BLK), 0)
                probs = jnp.where(at <= limit - chunk * CHUNK, probs, 0.0)
            d_probs = dot_nt(v_ref[rows, :], grads)
            d_scores = (probs * (d_probs - center) * (1.0 - ratio * ratio)).astype(BF16)
            d_values[rows, :] += dot(probs.astype(BF16), grads)
            d_keys[rows, :] += dot(d_scores, queries)
            acc[...] += dot(keys_t[chunk], d_scores)

        over_chunks(step, whole_chunks(meta, t), chunks)
        turned = acc[...].T * HD ** (-0.5)
        for i, (block, place) in enumerate(((b0, 80 + 2 * t), (b1, 81 + 2 * t))):
            cosine, sine = block_tables(tables, meta[place])
            for h in range(2):
                part = turned[(2 * h + i) * BLK : (2 * h + i + 1) * BLK]
                first, second = part[:, :HALF], part[:, HALF:]
                dq_ref[block_rows(block), h * HD : h * HD + HALF] = (
                    first * cosine + second * sine
                ).astype(BF16)
                dq_ref[block_rows(block), h * HD + HALF : (h + 1) * HD] = (
                    second * cosine - first * sine
                ).astype(BF16)
        return carry

    lax.fori_loop(0, 4, tile, 0)

    def finish(chunk, carry):
        rows = rows_of(chunk)
        cosine, sine = chunk_tables(tables, chunk)
        first, second = d_keys[rows, :HALF], d_keys[rows, HALF:]
        d_both[rows, :HALF] = (first * cosine + second * sine).astype(BF16)
        d_both[rows, HALF:HD] = (second * cosine - first * sine).astype(BF16)
        d_both[rows, HD:] = d_values[rows, :].astype(BF16)
        return carry

    lax.fori_loop(0, needed, finish, 0)

    def clear(chunk, carry):
        d_both[rows_of(chunk), :] = jnp.zeros((CHUNK, 2 * HD), BF16)
        return carry

    lax.fori_loop(needed, 8, clear, 0)
    for n in range(16):
        for b in range(4):
            target = near_ref.at[n] if n < 8 else far_ref.at[n - 8]
            pltpu.make_async_copy(
                d_both.at[block_rows(meta[n * 4 + b]), :], target.at[pl.ds(b * BLK, BLK), :], out_sem
            ).start()

    whole = pltpu.make_async_copy(d_both, both_ref, both_sem)
    whole.start()
    q_next = qkv_next[: q_own.shape[0], :HD]
    partial = dot_nt(dq_ref[:, :HD], q_own[...]) + dot_nt(dq_ref[:, HD:], q_next)
    dn_own[...] = partial[: 4 * BLK]
    dn_give[...] = partial[4 * BLK :].astype(BF16)
    whole.wait()
    pltpu.make_async_copy(d_both, d_both, out_sem).wait()


def proj_grads_kernel(meta, dq, q_own, qkv_next, kv_w, gains, gain_in, both_in, n_in, terms_ref, give_ref, *refs):
    normed, both, normed_q, kv_grad, n_sem, b_sem = refs
    loads = [pltpu.make_async_copy(both_in, both, b_sem), pltpu.make_async_copy(n_in, normed, n_sem)]
    for load in loads:
        load.start()
    for load in loads:
        load.wait()
    kv_grad[...] = jnp.zeros_like(kv_grad)

    def add(chunk, carry):
        rows = rows_of(chunk)
        kv_grad[...] += dot_tn(both[rows, :], normed[rows, :])
        return carry

    lax.fori_loop(0, chunks_needed(meta), add, 0)
    for b in range(8):
        normed_q[b * BLK : (b + 1) * BLK, :] = normed[block_rows(q_block(meta, b)), :]
    q_next = qkv_next[: q_own.shape[0], :HD]
    weighed = jnp.sum(kv_grad[...] * kv_w[...].T.astype(F32), axis=0, keepdims=True)
    for h, weight in enumerate((q_own[...], q_next)):
        q_grad = dot_tn(dq[:, h * HD : (h + 1) * HD], normed_q[...])
        weighed = weighed + jnp.sum(q_grad * weight.T.astype(F32), axis=0, keepdims=True)
        terms_ref[h, :HD, :] = q_grad
    gain_rows = jnp.concatenate(
        [weighed / (1.0 + gains[0:1, :]), gain_in[1:8, :], jnp.zeros((8, gains.shape[1]), F32)], axis=0
    )
    yh, c = meta[65], meta[66]
    quarter = HD // 4
    for h in range(2):
        side = yh if h == 0 else 1 - yh
        for kv in range(2):
            mine = pl.ds(pl.multiple_of(kv * HD + (2 * side + c) * quarter, quarter), quarter)
            theirs = pl.ds(pl.multiple_of(kv * HD + (2 * side + 1 - c) * quarter, quarter), quarter)
            terms_ref[h, HD + kv * quarter : HD + (kv + 1) * quarter, :] = kv_grad[mine, :]
            at = h * 2 * quarter + kv * quarter
            give_ref[at : at + quarter, :] = kv_grad[theirs, :].astype(BF16)
        terms_ref[h, HD + 2 * quarter : HD + 2 * quarter + 16, :] = gain_rows
        terms_ref[h, HD + 2 * quarter + 16 :, :] = jnp.zeros((2 * quarter - 16, gains.shape[1]), F32)
    give_ref[4 * quarter :, :] = gain_rows.astype(BF16)


def attend(meta, weights, gains, tables, pieces, after):
    width = pieces[0].shape[1]
    return pl.pallas_call(
        functools.partial(attend_kernel, len(after)),
        out_shape=(
            shape((2, 8, BLK, HD), BF16),
            shape((2, 4 * BLK, HD), BF16),
            shape((2, 4 * BLK, HD), BF16),
            shape((4, HD, 4 * BLK), BF16),
            shape((4, 8, 4 * BLK), F32),
            shape((width, 2 * HD), BF16),
            shape((SLOTS, width), BF16),
            shape((SLOTS, HD), BF16),
            shape((SLOTS, HD), BF16),
        ),
        in_specs=[SMEM_SPEC] + [VMEM_SPEC] * 6 + [ANY_SPEC] * (10 + len(after)),
        out_specs=(VMEM_SPEC,) * 6 + (HBM_SPEC,) * 3,
        scratch_shapes=[
            pltpu.VMEM((SLOTS, width), BF16),
            pltpu.VMEM((8 * BLK, width), BF16),
            pltpu.VMEM((SLOTS, HD), BF16),
            pltpu.VMEM((SLOTS, HD), BF16),
            pltpu.VMEM((SLOTS // CHUNK, HD, CHUNK), BF16),
            pltpu.VMEM((HD, 4 * BLK), F32),
            pltpu.VMEM((8, 4 * BLK), F32),
            DMA,
            DMA,
            DMA,
            DMA,
        ],
        compiler_params=params(VMEM),
        cost_estimate=cost(20, 20),
        name="attend",
    )(meta, *weights, gains, tables, *pieces, *after)


def attend_back(meta, queries, d_own, pack_oth, mixed_t, inverse, weights, tables, keys, values, after):
    width = weights[0].shape[0]
    rows = 4 * BLK
    return pl.pallas_call(
        attend_back_kernel,
        out_shape=(
            shape((2 * rows, 2 * HD), BF16),
            shape((SLOTS, 2 * HD), BF16),
            shape((rows, width), F32),
            shape((rows, width), BF16),
            shape((8, rows, 2 * HD), BF16),
            shape((8, rows, 2 * HD), BF16),
        ),
        in_specs=[SMEM_SPEC] + [VMEM_SPEC] * 2 + [ANY_SPEC] + [VMEM_SPEC] * 5 + [HBM_SPEC] * 2 + [ANY_SPEC],
        out_specs=(VMEM_SPEC, HBM_SPEC, VMEM_SPEC, VMEM_SPEC, ANY_SPEC, ANY_SPEC),
        scratch_shapes=[
            pltpu.VMEM((2, 8, BLK, HD), BF16),
            pltpu.VMEM((rows, 2 * HD), BF16),
            pltpu.VMEM((SLOTS, HD), BF16),
            pltpu.VMEM((SLOTS, HD), BF16),
            pltpu.VMEM((SLOTS // CHUNK, HD, CHUNK), BF16),
            pltpu.VMEM((SLOTS, HD), F32),
            pltpu.VMEM((SLOTS, HD), F32),
            pltpu.VMEM((SLOTS, 2 * HD), BF16),
            pltpu.VMEM((HD, 4 * BLK), F32),
            DMA,
            DMA,
            DMA,
            DMA,
            DMA,
        ],
        compiler_params=params(VMEM),
        cost_estimate=cost(40, 30),
        name="attend_back",
    )(meta, queries, d_own, pack_oth, mixed_t, inverse, *weights, tables, keys, values, *after)


def proj_grads(meta, dq, weights, gains, gain_in, both, normed):
    width = normed.shape[1]
    return pl.pallas_call(
        proj_grads_kernel,
        out_shape=(shape((2, 2 * HD, width), F32), shape((HD + 16, width), BF16)),
        in_specs=[SMEM_SPEC] + [VMEM_SPEC] * 6 + [HBM_SPEC] * 2,
        out_specs=(VMEM_SPEC,) * 2,
        scratch_shapes=[
            pltpu.VMEM((SLOTS, width), BF16),
            pltpu.VMEM((SLOTS, 2 * HD), BF16),
            pltpu.VMEM((8 * BLK, width), BF16),
            pltpu.VMEM((2 * HD, width), F32),
            DMA,
            DMA,
        ],
        compiler_params=params(VMEM),
        cost_estimate=cost(2, 12),
        name="proj_grads",
    )(meta, dq, *weights, gains, gain_in, both, normed)


GELU_A, GELU_B = 0.7978845608028654, 0.044715


def feed_kernel(meta, gains, mix_own, mix_oth, tok0, tok1, cot0, cot1, *refs):
    weights = refs[:8]
    result0, result1, d_middle_ref, keep_mix, pack, keep, gain_ref = refs[8:15]
    wdo, wgu, zs, sems = refs[15:]
    rows, width = 2 * tok0.shape[0], tok0.shape[1]
    hid = wgu.shape[2] // 2
    copies = [pltpu.make_async_copy(weights[s], wdo.at[s], sems.at[s]) for s in range(4)]
    copies += [pltpu.make_async_copy(weights[4 + s], wgu.at[s], sems.at[4 + s]) for s in range(4)]
    for copy in copies:
        copy.start()
    gain_b, gain_c, gain_d = gains[1:2, :], gains[2:3, :], gains[3:4, :]
    valid = []
    for b in range(4):
        inner = lax.broadcasted_iota(jnp.int32, (BLK, 1), 0)
        valid.append(meta[b] * BLK + inner < meta[64])
    valid = jnp.concatenate([v.astype(F32) for v in valid], axis=0) > 0.5
    start = jnp.concatenate([tok0[...].astype(F32), tok1[...].astype(F32)], axis=0)
    branch = jnp.zeros((rows, width), F32)
    for s in range(4):
        copies[s].wait()
        mixed = mix_own[s] if s < 2 else mix_oth[s - 2]
        branch = branch + dot(mixed, wdo[s, hid:, :])
    middle = start + branch * inverse_rms(branch) * (1.0 + gain_b)
    second = (middle * inverse_rms(middle) * (1.0 + gain_c)).astype(BF16)
    pack[:, :width] = second
    output = jnp.zeros((rows, width), F32)
    at = 3 * width
    for s in range(4):
        copies[4 + s].wait()
        both = dot(second, wgu[s])
        zs[s] = both
        gate, up = both[:, :hid], both[:, hid:]
        bent = jnp.tanh(GELU_A * (gate + GELU_B * gate * gate * gate))
        hidden = (0.5 * gate * (1.0 + bent) * up).astype(BF16)
        if s < 2:
            keep[:, s * hid : (s + 1) * hid] = hidden
        else:
            pack[:, at + (s - 2) * hid : at + (s - 1) * hid] = hidden
        output = output + dot(hidden, wdo[s, :hid, :])
    result = jnp.where(
        valid, middle + output * inverse_rms(output) * (1.0 + gain_d), 0.0
    ).astype(BF16)
    result0[...] = result[: rows // 2]
    result1[...] = result[rows // 2 :]
    cot = jnp.concatenate([cot0[...].astype(F32), cot1[...].astype(F32)], axis=0)
    seed = jnp.where(valid, cot, 0.0)
    d_output, d_gain_d = norm_back(output, gain_d, seed)
    d_output = d_output.astype(BF16)
    pack[:, width : 2 * width] = d_output
    d_second = jnp.zeros((rows, width), F32)
    for s in range(4):
        d_hidden = dot_nt(d_output, wdo[s, :hid, :])
        gate, up = zs[s, :, :hid], zs[s, :, hid:]
        square = gate * gate
        bent = jnp.tanh(GELU_A * gate * (1.0 + GELU_B * square))
        slope = 0.5 * (1.0 + bent) + (0.5 * GELU_A) * gate * (1.0 - bent * bent) * (
            1.0 + 3.0 * GELU_B * square
        )
        d_gate = (d_hidden * up * slope).astype(BF16)
        d_up = (d_hidden * (0.5 * gate * (1.0 + bent))).astype(BF16)
        if s < 2:
            where = 2 * hid + s * 2 * hid
            keep[:, where : where + hid] = d_gate
            keep[:, where + hid : where + 2 * hid] = d_up
        else:
            where = at + 2 * hid + (s - 2) * 2 * hid
            pack[:, where : where + hid] = d_gate
            pack[:, where + hid : where + 2 * hid] = d_up
        d_second = d_second + dot_nt(d_gate, wgu[s, :, :hid]) + dot_nt(d_up, wgu[s, :, hid:])
    d_mid, d_gain_c = norm_back(middle, gain_c, d_second)
    d_middle = seed + d_mid
    d_middle_ref[...] = d_middle
    d_branch, d_gain_b = norm_back(branch, gain_b, d_middle)
    d_branch = d_branch.astype(BF16)
    pack[:, 2 * width : 3 * width] = d_branch
    for s in range(4):
        d_mixed = dot_nt(d_branch, wdo[s, hid:, :]).astype(BF16)
        if s < 2:
            keep_mix[s] = d_mixed
        else:
            pack[:, at + 6 * hid + (s - 2) * HD : at + 6 * hid + (s - 1) * HD] = d_mixed
    zero = jnp.zeros((1, width), F32)
    gain_ref[...] = jnp.concatenate(
        [zero, d_gain_b[None], d_gain_c[None], d_gain_d[None], zero, zero, zero, zero], axis=0
    )


def feed(meta, gains, mix_own, mix_oth, tok, cot, do_weights, gu_weights):
    rows, width = 2 * tok[0].shape[0], tok[0].shape[1]
    hid = gu_weights[0].shape[1] // 2
    do_rows = do_weights[0].shape[0]
    return pl.pallas_call(
        feed_kernel,
        out_shape=(
            shape((rows // 2, width), BF16),
            shape((rows // 2, width), BF16),
            shape((rows, width), F32),
            shape((2, rows, HD), BF16),
            shape((rows, 3 * width + 6 * hid + 2 * HD), BF16),
            shape((rows, 6 * hid), BF16),
            shape((8, width), F32),
        ),
        in_specs=[SMEM_SPEC] + [VMEM_SPEC] * 7 + [ANY_SPEC] * 8,
        out_specs=(VMEM_SPEC,) * 7,
        scratch_shapes=[
            pltpu.VMEM((4, do_rows, width), BF16),
            pltpu.VMEM((4, width, 2 * hid), BF16),
            pltpu.VMEM((4, rows, 2 * hid), F32),
            pltpu.SemaphoreType.DMA((8,)),
        ],
        compiler_params=params(VMEM),
        cost_estimate=cost(5, 16),
        name="feed",
    )(meta, gains, mix_own, mix_oth, *tok, *cot, *do_weights, *gu_weights)


QKV = 32


def feed_grads_kernel(own, oth, keep, mix_own, mix_oth, out_ref):
    hid = keep.shape[1] // 6
    share, width = out_ref.shape[3:]
    at = 3 * width

    def put(s, first, value):
        row, last = first, first + value.shape[0]
        while row < last:
            to, inner = row // share, row % share
            count = min(last - row, share - inner)
            part = value[row - first : row - first + count]
            out_ref[to % 4, to // 4, s, inner : inner + count, :] = part
            row += count

    for s in range(2):
        for part in range(2):
            mine = 2 * hid + (2 * s + part) * hid
            theirs = at + 2 * hid + (2 * s + part) * hid
            value = dot_tn(keep[:, mine : mine + hid], own[:, :width])
            value = value + dot_tn(oth[:, theirs : theirs + hid], oth[:, :width])
            put(s, part * hid, value.astype(BF16))
        value = dot_tn(keep[:, s * hid : (s + 1) * hid], own[:, width : 2 * width])
        value = value + dot_tn(oth[:, at + s * hid : at + (s + 1) * hid], oth[:, width : 2 * width])
        put(s, 2 * hid, value.astype(BF16))
        value = dot_tn(mix_own[s], own[:, 2 * width : 3 * width])
        value = value + dot_tn(mix_oth[s], oth[:, 2 * width : 3 * width])
        put(s, 3 * hid, value.astype(BF16))


def share_sum_kernel(got, *outs):
    for s, out in enumerate(outs):
        total = got[0, s].astype(F32)
        for n in range(1, 16):
            total = total + got[n, s].astype(F32)
        out[...] = total.astype(BF16)


def total_kernel(a, b, c, d, out):
    total = a[...].astype(F32) + b[...].astype(F32) + c[...].astype(F32) + d[...].astype(F32)
    out[...] = total.astype(BF16)


def total_wide_kernel(a, b, c, d, out):
    total = a[...].astype(F32) + b[...].astype(F32) + c[...].astype(F32) + d[...].astype(F32)
    out[...] = jnp.broadcast_to(total.astype(BF16)[None], out.shape)


def feed_out_kernel(got, gate, up, down, out):
    hid = gate.shape[1]
    whole = jnp.concatenate([got[n].astype(F32) for n in range(16)], axis=0)
    gate[...] = whole[:hid].T
    up[...] = whole[hid : 2 * hid].T
    down[...] = whole[2 * hid : 3 * hid]
    out[...] = whole[3 * hid :]


def qkv_out_kernel(got, q_out, k_out, v_out, gain_out):
    small = jnp.concatenate([got[n].astype(F32) for n in range(16)], axis=0)
    quarter = HD // 4
    q_out[...] = small[:HD].T
    k_out[...] = small[HD : HD + quarter]
    v_out[...] = small[HD + quarter : HD + 2 * quarter]
    gain_out[...] = small[HD + 2 * quarter : HD + 2 * quarter + 8]


def sum_a_kernel(near, far, g0, g1, k0, k1):
    gives, keeps = (g0, g1), (k0, k1)
    for p, (first, last, (a, b, d)) in enumerate(BACK_PARTS):
        size = last - first
        for i, move in enumerate((0, a, b, a | b)):
            rows = pl.ds(i * size, size)
            for out, at in ((keeps[p], move), (gives[p], move | d)):
                both = near[at, first:last].astype(F32) + far[at, first:last].astype(F32)
                out[rows, :] = both.astype(out.dtype)


def qkv_shares_kernel(terms, got, shares):
    half = HD // 2
    for h in range(2):
        for n in range(16):
            at = n * QKV
            value = terms[h, at : at + QKV]
            if HD <= at < HD + half:
                from_row = h * half + at - HD
                value = value + got[from_row : from_row + QKV].astype(F32)
            if at == HD + half:
                rest = jnp.zeros((QKV - 16, terms.shape[2]), F32)
                value = value + jnp.concatenate([got[HD:].astype(F32), rest], axis=0)
            shares[n, h] = value.astype(BF16)


def halves(keeps, gots, outs):
    for p in range(2):
        rows = keeps[p].shape[0] // 2
        outs[p][...] = (keeps[p][rows:] + gots[p][rows:].astype(F32)).astype(BF16)
        outs[2 + p][...] = keeps[p][:rows] + gots[p][:rows].astype(F32)


def sum_b_kernel(k0, k1, g0, g1, *outs):
    halves((k0, k1), (g0, g1), outs)


def sum_d_kernel(k0, k1, g0, g1, dn, dn_got, tok0, tok1, d_middle, kv_w, gains, t0, t1):
    d_kv = [k[...] + g[...].astype(F32) for k, g in ((k0, g0), (k1, g1))]
    d_kv = jnp.concatenate(d_kv, axis=0).astype(BF16)
    d_normed = dn[...] + dn_got[...].astype(F32) + dot_nt(d_kv, kv_w[...])
    start = jnp.concatenate([tok0[...].astype(F32), tok1[...].astype(F32)], axis=0)
    d_start, _ = norm_back(start, gains[0:1, :], d_normed)
    grads = (d_middle[...] + d_start).astype(BF16)
    half = t0.shape[0]
    t0[...] = grads[:half]
    t1[...] = grads[half:]


def on_device(
    tokens,
    cotangent,
    lengths,
    block_order,
    query_weight,
    key_weight,
    value_weight,
    out_weight,
    gate_weight,
    up_weight,
    down_weight,
    gain_attn_in,
    gain_attn_out,
    gain_ffn_in,
    gain_ffn_out,
):
    ctx, fsdp = lax.axis_index("ctx"), lax.axis_index("fsdp")
    yl, z, x = ctx // 16, (ctx // 4) % 4, ctx % 4
    yh, c = fsdp // 2, fsdp % 2
    zh, zl, xh, xl = z // 2, z % 2, x // 2, x % 2
    low_y, low_c, low_x = yh == 0, c == 0, xh == 0
    own_rows = 4 * BLK
    width = tokens.shape[-1]

    def rows_to(array):
        return (
            send(jnp.where(low_x, array[0, 0], array[0, 1]), regroup(0)),
            send(jnp.where(low_x, array[0, 1], array[0, 0]), regroup(1)),
        )

    def rows_back(first, second):
        first, second = send(first, regroup(0)), send(second, regroup(1))
        return jnp.stack([jnp.where(low_x, first, second), jnp.where(low_x, second, first)])[None]

    tok0, tok1 = rows_to(tokens)
    part_shapes = [shape((size, width), BF16) for size in sizes()]
    spot = jnp.stack([yh, c, zh, zl, xh, xl, yl, fsdp]).astype(jnp.int32)
    part_shapes = [shape((size, width), BF16) for size in sizes()]
    heads = HD
    quarter = key_weight.shape[1]
    hidden_cols = gate_weight.shape[1]
    share = gain_attn_in.shape[0]
    length_parts = jnp.concatenate([lengths // 64, lengths % 64], axis=0).astype(BF16)
    gains = jnp.stack([gain_attn_in, gain_attn_out, gain_ffn_in, gain_ffn_out])
    gains = jnp.concatenate([gains, jnp.pad(length_parts, ((0, 0), (0, share - 2)))], axis=0)
    (qkv_own,) = step(
        pack_qkv_kernel,
        [shape((width + 16, heads + 2 * quarter), BF16)],
        (query_weight, key_weight.T, value_weight.T, gains),
        mbytes=6,
        name="pack_qkv",
    )
    qkv_next = send(qkv_own, to_next)
    parts = step(cut_kernel, part_shapes, (tok0, tok1), after=(qkv_own,), mbytes=6, name="cut")

    def cube_send(arrays, stage):
        return [send(array, to_cube(order[stage])) for array, (first, last, order) in zip(arrays, PARTS)]

    got = cube_send(parts, 0)

    (do_own,) = step(
        pack_rows_kernel,
        [shape((hidden_cols + heads, width), BF16)],
        (down_weight, out_weight),
        after=(parts[0],),
        name="pack_do",
    )
    do_next = send(do_own, to_next)
    pairs = step(
        functools.partial(join_kernel, 3),
        [shape((2 * size, width), BF16) for size in sizes()],
        (*parts, *got),
        after=(do_own,),
        mbytes=6,
        name="join",
    )
    got = cube_send(pairs, 1)

    (kv_pair,) = step(
        kv_pair_kernel,
        [shape((width + 32, 4 * quarter), BF16)],
        (qkv_own, qkv_next),
        meta=spot,
        mbytes=6,
        name="kv_pair",
    )
    kv_other = send(kv_pair, to_core)
    mine, theirs = (
        m[width:, :share].reshape(2, 16, share)[:, :6] for m in (kv_pair, kv_other)
    )
    quarters = jnp.stack(
        [jnp.where(low_c, mine, theirs), jnp.where(low_c, theirs, mine)], axis=1
    )
    all_gains = jnp.transpose(quarters[:, :, :4], (2, 0, 1, 3)).reshape(4, width).astype(F32)
    gain_rows = jnp.concatenate([all_gains, jnp.zeros((4, width), F32)], axis=0)
    lengths_here = jnp.where(low_y, quarters[0, :, 4:, :2], quarters[1, :, 4:, :2])
    lengths_here = jnp.where(zh == 0, lengths_here[0], lengths_here[1]).astype(jnp.int32)
    lengths_here = lengths_here[0] * 64 + lengths_here[1]
    length = jnp.where(low_x, lengths_here[0], lengths_here[1])

    joined = step(
        join_all_kernel,
        [shape((4 * size, width), BF16) for size in sizes()] + [shape((4 * own_rows, width), BF16)],
        (*pairs, *got),
        after=(kv_pair,),
        mbytes=8,
        name="join_all",
    )
    low_parts, low_all = joined[:3], joined[3]
    high_parts = cube_send(low_parts, 2)
    (gu_own,) = step(
        pack_columns_kernel,
        [shape((width, 2 * hidden_cols), BF16)],
        (gate_weight, up_weight),
        after=(do_next, high_parts[0]),
        name="pack_gu",
    )

    stored = []
    for other in range(2):
        for move in range(8):
            dy, dz, dx = move >> 2, (move >> 1) & 1, move & 1
            for turn in range(2):
                place = (yl ^ dy) * 16 + ((c ^ other) * 2 + (zl ^ dz)) * 4
                place = place + (xh ^ turn) * 2 + (xl ^ dx)
                stored += [place * 2, place * 2 + 1]
    stored = jnp.stack(stored)
    slots = jnp.arange(64, dtype=jnp.int32)
    block_at = jnp.sum(
        jnp.where(stored[:, None] == slots[None, :], block_order[None, :], 0), axis=1
    ).astype(jnp.int32)
    q_blocks = jnp.concatenate([block_at[0:4], block_at[32:36]])
    rank = jnp.sum((q_blocks[None, :] < q_blocks[:, None]).astype(jnp.int32), axis=1)
    eight = jnp.arange(8, dtype=jnp.int32)
    chosen = rank[None, :] == eight[:, None]
    order = jnp.sum(jnp.where(chosen, eight[None, :], 0), axis=1).astype(jnp.int32)
    order_block = jnp.sum(jnp.where(chosen, q_blocks[None, :], 0), axis=1).astype(jnp.int32)
    facts = jnp.stack([length, yh, c, zh, xh, x, z, z]).astype(jnp.int32)
    meta = jnp.concatenate([block_at, facts, order, order_block])

    low_all = send(low_all, to_core)
    high_far = [send(part, to_core) for part in high_parts]
    pieces = list(low_parts) + high_parts + [low_all] + high_far
    tables = jnp.asarray(angle_tables())
    gu_next = send(gu_own, to_next)
    (do_late,) = gate((do_own,), (high_parts[2],))
    do_swap, do_next_swap = send(do_late, to_core), send(do_next, to_core)
    do_weights = [do_late, do_next, do_swap, do_next_swap]
    gu_swap = send(gu_own, to_core)
    half_shape = shape((own_rows // 2, width), BF16)
    cot0, cot1 = step(
        pick_kernel,
        [half_shape, half_shape],
        (cotangent[0],),
        after=(joined[0],),
        meta=spot,
        mbytes=6,
        name="pick_cot",
    )
    cot0, cot1 = send(cot0, regroup(0)), send(cot1, regroup(1))
    queries, mix_own, mix_oth, mixed_t, inverse, kv_weight, sorted_normed, keys, values = attend(
        meta, (query_weight, qkv_next, kv_pair, kv_other), gain_rows, tables, pieces, (do_swap, do_next_swap, gu_swap)
    )

    (gu_next,) = gate((gu_next,), (mix_own, cot0, cot1))
    gu_weights = [gu_own, gu_next, gu_swap, send(gu_next, to_core)]
    result0, result1, d_middle, keep_mix, pack, keep, gain_terms = feed(
        meta, gain_rows, mix_own, send(mix_oth, to_core), (tok0, tok1), (cot0, cot1), do_weights, gu_weights
    )
    pack_oth = send(pack, to_core)
    span = 3 * hidden_cols + HD
    (feed_shares,) = step(
        feed_grads_kernel,
        [shape((4, 4, 2, span // 16, width), BF16)],
        (pack, pack_oth, keep, mix_own, mix_oth),
        name="feed_grads",
    )
    feed_sums = lax.psum_scatter(feed_shares, "ctx", scatter_dimension=0, axis_index_groups=ROWS)

    dq, d_both, dn_own, dn_give, d_near, d_far = attend_back(
        meta,
        queries,
        keep_mix,
        pack_oth,
        mixed_t,
        inverse,
        (query_weight, qkv_next),
        tables,
        keys,
        values,
        (feed_shares,),
    )
    d_far, dn_got = send(d_far, to_core), send(dn_give, to_core)

    def part_shape(count, dtype):
        return [shape((count * (last - first), 2 * HD), dtype) for first, last, order in BACK_PARTS]

    def rows_shape(*dims):
        return shape((*dims, width), BF16)

    def cube_return(arrays, stage):
        return [
            send(array, to_cube(order[stage])) for array, (first, last, order) in zip(arrays, BACK_PARTS)
        ]

    def over_y(mine, theirs):
        return mine, send(mine, to_yl), send(theirs, to_next), send(theirs, to_yh)

    outs = step(
        sum_a_kernel, part_shape(4, BF16) + part_shape(4, F32), (d_near, d_far), name="sum_a"
    )
    got, keeps = cube_return(outs[:2], 2), outs[2:4]
    terms, core_give = proj_grads(
        meta, dq, (query_weight, qkv_next, kv_weight), gain_rows, gain_terms, d_both, sorted_normed
    )
    core_got = send(core_give, to_core)
    (qkv_shares,) = step(
        qkv_shares_kernel, [rows_shape(16, 2, QKV)], (terms, core_got), name="qkv_shares"
    )
    (feed_sums,) = gate((feed_sums,), (qkv_shares,))
    feed_sums = lax.psum_scatter(feed_sums, "ctx", scatter_dimension=0, axis_index_groups=COLUMNS)
    outs = step(
        sum_b_kernel,
        part_shape(2, BF16) + part_shape(2, F32),
        (*keeps, *got),
        after=(qkv_shares,),
        name="sum_b",
    )
    got, keeps = cube_return(outs[:2], 1), outs[2:4]
    outs = step(
        sum_b_kernel, part_shape(1, BF16) + part_shape(1, F32), (*keeps, *got), name="sum_c"
    )
    got, keeps = cube_return(outs[:2], 0), outs[2:4]
    (feed_sums,) = gate((feed_sums,), (outs[0],))
    feed_terms = over_y(feed_sums[0], feed_sums[1])
    (feed_all,) = step(
        total_kernel, [rows_shape(span // 16)], feed_terms, after=(*got,), name="feed_total"
    )
    (qkv_shares,) = gate((qkv_shares,), (feed_all,))
    qkv_got = swap_plane(qkv_shares)
    feed_all = lax.all_gather(feed_all, "ctx", axis_index_groups=PLANE)
    tok_back0, tok_back1 = step(
        sum_d_kernel,
        [rows_shape(own_rows // 2)] * 2,
        (*keeps, *got, dn_own, dn_got, tok0, tok1, d_middle, kv_weight, gain_rows),
        after=(qkv_shares,),
        name="sum_d",
    )
    token_block = rows_back(tok_back0, tok_back1).astype(F32)
    mine, theirs = step(
        share_sum_kernel, [rows_shape(QKV)] * 2, (qkv_got,), after=(tok_back0,), name="qkv_sum"
    )
    qkv_terms = over_y(mine, theirs)
    (qkv_all,) = step(total_wide_kernel, [rows_shape(16, QKV)], qkv_terms, name="qkv_total")
    result0, result1 = gate((result0, result1), (mine,))
    result_block = rows_back(result0, result1)
    qkv_all = swap_plane(qkv_all)
    q_grad, k_grad, v_grad, gain_sum = step(
        qkv_out_kernel,
        [
            shape((width, HD), F32),
            shape((quarter, width), F32),
            shape((quarter, width), F32),
            shape((8, width), F32),
        ],
        (qkv_all,),
        name="qkv_out",
    )
    gate_grad, up_grad, down_grad, out_grad = step(
        feed_out_kernel,
        [
            shape((width, hidden_cols), F32),
            shape((width, hidden_cols), F32),
            shape((hidden_cols, width), F32),
            shape((HD, width), F32),
        ],
        (feed_all,),
        name="feed_out",
    )
    share_rows = width // 4
    gain_grads = lax.dynamic_slice_in_dim(gain_sum, fsdp * share_rows, share_rows, axis=1)
    return (
        result_block,
        token_block,
        q_grad,
        k_grad.T,
        v_grad.T,
        out_grad,
        gate_grad,
        up_grad,
        down_grad,
        gain_grads[0],
        gain_grads[1],
        gain_grads[2],
        gain_grads[3],
    )


def solution(mesh):
    rows, cols, first = P("fsdp", None, "ctx", None), P(None, "fsdp"), P("fsdp", None)
    weights = (cols, cols, cols, first, cols, cols, first)
    gains = (P("fsdp"),) * 4
    return jax.shard_map(
        on_device,
        mesh=mesh,
        in_specs=(rows, rows, first, P()) + weights + gains,
        out_specs=(rows, rows) + weights + gains,
        check_vma=False,
    )
```

```python
import functools

import jax
import jax.numpy as jnp
import numpy as np
from jax import lax
from jax.experimental import pallas as pl
from jax.experimental.pallas import tpu as pltpu
from jax.sharding import PartitionSpec as P

F32, BF16 = jnp.float32, jnp.bfloat16
CAP = 50.0
CAP_LOG2 = CAP * 1.4426950408889634
EPS = 1e-06
BASE = 1000000.0
HD = 256
HALF = HD // 2
BLK = 64
CHUNK = 2048
VMEM = 54
AXES = ("ctx", "fsdp")


def all_places():
    for yl in range(2):
        for z in range(4):
            for x in range(4):
                for yh in range(2):
                    for c in range(2):
                        yield yl, z, x, yh, c


def flat(yl, z, x, yh, c):
    return (((yl * 4 + z) * 4 + x) * 2 + yh) * 2 + c


def send(array, move):
    pairs = [(flat(*p), flat(*move(*p))) for p in all_places()]
    return lax.ppermute(array, AXES, pairs)


def to_core(yl, z, x, yh, c):
    return yl, z, x, yh, 1 - c


def to_next(yl, z, x, yh, c):
    return 1 - yl, z, x, 1 - yh, c


def to_yl(yl, z, x, yh, c):
    return 1 - yl, z, x, yh, c


def to_yh(yl, z, x, yh, c):
    return yl, z, x, 1 - yh, c


def to_zpair(yl, z, x, yh, c):
    return yl, z ^ 1, x, yh, c


def to_xpair(yl, z, x, yh, c):
    return yl, z, x ^ 1, yh, c


def to_zring(yl, z, x, yh, c):
    return yl, (z + (1 if z % 2 else 3)) % 4, x, yh, c


def to_xring(yl, z, x, yh, c):
    return yl, z, (x + (1 if x % 2 else 3)) % 4, yh, c


def regroup(turn):
    def move(yl, z, x, yh, c):
        zh, zl, xh, xl = z // 2, z % 2, x // 2, x % 2
        return yl, c * 2 + zl, (xh ^ turn) * 2 + xl, yh, zh

    return move


def to_cube(step):
    dy, dz, dx = step >> 2, (step >> 1) & 1, step & 1

    def move(yl, z, x, yh, c):
        return yl ^ dy, z ^ dz, x ^ dx, yh, c

    return move


PARTS = ((0, 96, (4, 2, 1)), (96, 176, (2, 1, 4)), (176, 256, (1, 4, 2)))


BACK_PARTS = ((0, 128, (4, 2, 1)), (128, 256, (2, 1, 4)))


def held_by(order):
    a, b, d = order
    low = (0, a, b, a | b)
    return low, tuple(d | step for step in low)


def copy_kernel(array, out):
    out[...] = array[...]


def pack_rows_kernel(first, second, out):
    out[: first.shape[0]] = first[...]
    out[first.shape[0] :] = second[...]


def pack_columns_kernel(first, second, out):
    out[:, : first.shape[1]] = first[...]
    out[:, first.shape[1] :] = second[...]


def pack_qkv_kernel(query, key_t, value_t, gains, out):
    rows, width = query.shape[0], gains.shape[1]
    out[:rows, :HD] = query[...]
    out[:rows, HD:] = jnp.concatenate([key_t[...], value_t[...]], axis=0).T
    out[rows:, :] = jnp.zeros((out.shape[0] - rows, out.shape[1]), BF16)
    out[rows : rows + gains.shape[0], :width] = gains[...]


def kv_pair_kernel(spot, own, after, out):
    low = spot[0] == 0
    half = HD // 2
    rows = own.shape[0] - 16
    mine, theirs = own[:rows, HD:], after[:rows, HD:]
    out[:rows, :half] = jnp.where(low, mine, theirs)
    out[:rows, half:] = jnp.where(low, theirs, mine)
    mine, theirs = own[rows:, :HD], after[rows:, :HD]
    out[rows : rows + 16, :] = jnp.where(low, mine, theirs)
    out[rows + 16 :, :] = jnp.where(low, theirs, mine)


def pick_kernel(spot, array, first, second):
    low = spot[4] == 0
    first[...] = jnp.where(low, array[0], array[1])
    second[...] = jnp.where(low, array[1], array[0])


def sizes():
    return [last - first for first, last, order in PARTS]


def cut_kernel(r0, r1, *outs):
    half = r0.shape[0]
    for (first, last, order), out in zip(PARTS, outs):
        if first < half:
            out[: min(last, half) - first] = r0[first : min(last, half)]
        if last > half:
            out[max(first, half) - first :] = r1[max(first, half) - half : last - half]


def join_kernel(count, *refs):
    ins, outs = refs[: 2 * count], refs[-count:]
    for p in range(count):
        rows = ins[p].shape[0]
        outs[p][:rows] = ins[p][...]
        outs[p][rows:] = ins[count + p][...]


def join_all_kernel(*refs):
    ins, outs = refs[:6], refs[-4:]
    at = 0
    for p in range(3):
        rows = ins[p].shape[0]
        outs[p][:rows] = ins[p][...]
        outs[p][rows:] = ins[3 + p][...]
        outs[3][at : at + rows] = ins[p][...]
        outs[3][at + rows : at + 2 * rows] = ins[3 + p][...]
        at += 2 * rows


PLANE = [[yl * 16 + i for i in range(16)] for yl in range(2)]


def swap_plane(array):
    return lax.all_to_all(
        array, "ctx", split_axis=0, concat_axis=0, axis_index_groups=PLANE, tiled=True
    )


def along_x(shift):
    def move(yl, z, x, yh, c):
        return yl, z, (x + shift) % 4, yh, c

    return move


def along_z(shift):
    def move(yl, z, x, yh, c):
        return yl, (z + shift) % 4, x, yh, c

    return move


def spread(arrays, along):
    return [send(array, along(r + 1)) for r, array in enumerate(arrays)]


ROWS = [[yl * 16 + z * 4 + x for x in range(4)] for yl in range(2) for z in range(4)]
COLUMNS = [[yl * 16 + z * 4 + x for z in range(4)] for yl in range(2) for x in range(4)]


def swap_z(array):
    return lax.all_to_all(
        array, "ctx", split_axis=0, concat_axis=0, axis_index_groups=COLUMNS, tiled=True
    )


def inverse_rms(values):
    return lax.rsqrt(jnp.mean(values * values, axis=-1, keepdims=True) + EPS)


def norm_back(values, gain, grads):
    scale = inverse_rms(values)
    hat = values * scale
    scaled = grads * (1.0 + gain)
    inner = jnp.mean(scaled * hat, axis=-1, keepdims=True)
    return scale * (scaled - hat * inner), jnp.sum(grads * hat, axis=0)


def dot(left, right):
    return jnp.dot(left, right, preferred_element_type=F32)


def dot_nt(left, right):
    return lax.dot_general(left, right, (((1,), (1,)), ((), ())), preferred_element_type=F32)


def dot_tn(left, right):
    return lax.dot_general(left, right, (((0,), (0,)), ((), ())), preferred_element_type=F32)


def angle_tables():
    freqs = BASE ** (-(np.arange(HALF, dtype=np.float32) * 2.0 / HD)).astype(np.float32)
    coarse = (np.arange(64, dtype=np.float64) * 64)[:, None] * freqs[None, :].astype(np.float64)
    fine = np.arange(BLK, dtype=np.float64)[:, None] * freqs[None, :].astype(np.float64)
    tables = [np.cos(coarse), np.sin(coarse), np.cos(fine), np.sin(fine)]
    return np.stack(tables).astype(np.float32)


SMEM_SPEC = pl.BlockSpec(memory_space=pltpu.SMEM)
VMEM_SPEC = pl.BlockSpec(memory_space=pltpu.VMEM)
ANY_SPEC = pl.BlockSpec(memory_space=pl.ANY)
HBM_SPEC = pl.BlockSpec(memory_space=pltpu.HBM)
DMA = pltpu.SemaphoreType.DMA
SLOTS = 4096


def shape(dims, dtype):
    return jax.ShapeDtypeStruct(dims, dtype)


def cost(gflops, mbytes):
    return pl.CostEstimate(
        flops=int(gflops * 10**9), bytes_accessed=int(mbytes * 10**6), transcendentals=0
    )


def params(mbytes):
    return pltpu.CompilerParams(vmem_limit_bytes=mbytes * 1024 * 1024)


def step(kernel, outs, arrays, after=(), meta=None, mbytes=VMEM, name=None, scratch=()):
    scalars = 0 if meta is None else 1
    used = scalars + len(arrays)

    def body(*refs):
        kernel(*refs[:used], *refs[used + len(after) :])

    return pl.pallas_call(
        body,
        out_shape=tuple(outs),
        in_specs=[SMEM_SPEC] * scalars + [VMEM_SPEC] * len(arrays) + [ANY_SPEC] * len(after),
        out_specs=(VMEM_SPEC,) * len(outs),
        scratch_shapes=list(scratch),
        compiler_params=params(mbytes),
        cost_estimate=cost(0.1, 4),
        name=name,
    )(*(() if meta is None else (meta,)), *arrays, *after)


def gate_kernel(*refs):
    pass


def gate(arrays, after):
    return pl.pallas_call(
        gate_kernel,
        out_shape=tuple(shape(a.shape, a.dtype) for a in arrays),
        in_specs=[ANY_SPEC] * (len(arrays) + len(after)),
        out_specs=(ANY_SPEC,) * len(arrays),
        input_output_aliases={i: i for i in range(len(arrays))},
        name="gate",
    )(*arrays, *after)


def chunk_tables(tables, chunk):
    rows = pl.ds(pl.multiple_of(chunk * (CHUNK // BLK), 8), CHUNK // BLK)
    ca = tables[0, rows, :][:, None, :]
    sa = tables[1, rows, :][:, None, :]
    cb = tables[2][None]
    sb = tables[3][None]
    cosine = (ca * cb - sa * sb).reshape(CHUNK, HALF)
    sine = (sa * cb + ca * sb).reshape(CHUNK, HALF)
    return cosine, sine


def block_tables(tables, block):
    ca, sa = tables[0, pl.ds(block, 1), :], tables[1, pl.ds(block, 1), :]
    cb, sb = tables[2], tables[3]
    return ca * cb - sa * sb, sa * cb + ca * sb


def tile_facts(meta, t):
    b0, b1 = meta[72 + 2 * t], meta[73 + 2 * t]
    p0, p1 = meta[80 + 2 * t], meta[81 + 2 * t]
    length = meta[64]
    last = jnp.minimum(p1 * BLK + BLK, length)
    chunks = jnp.where(p0 * BLK < length, (last + CHUNK - 1) // CHUNK, 0)
    lane = lax.broadcasted_iota(jnp.int32, (1, 4 * BLK), 1)
    second = (lane // BLK) % 2 == 1
    limit = jnp.where(second, p1, p0) * BLK + lane % BLK
    return b0, b1, chunks, jnp.minimum(limit, length - 1)


def whole_chunks(meta, t):
    return jnp.minimum(meta[80 + 2 * t] * BLK + 1, meta[64]) // CHUNK


def over_chunks(step, whole, chunks):
    def plain(chunk, carry):
        step(chunk, False)
        return carry

    def masked(chunk, carry):
        step(chunk, True)
        return carry

    first = jnp.minimum(whole, chunks)
    lax.fori_loop(0, first, plain, 0)
    lax.fori_loop(first, chunks, masked, 0)


def chunks_needed(meta):
    most = jnp.int32(0)
    for t in range(4):
        most = jnp.maximum(most, tile_facts(meta, t)[2])
    return most


def q_block(meta, b):
    return meta[b] if b < 4 else meta[28 + b]


def rows_of(chunk):
    return pl.ds(pl.multiple_of(chunk * CHUNK, CHUNK), CHUNK)


def block_rows(block):
    return pl.ds(pl.multiple_of(block * BLK, BLK), BLK)


def tile_rows(ref, b0, b1):
    return jnp.concatenate([ref[0, b0], ref[0, b1], ref[1, b0], ref[1, b1]], axis=0)


def put_tile(own, oth, b0, b1, tile):
    for block, rows in ((b0, 0), (b1, BLK)):
        for ref, base in ((own, 0), (oth, 4)):

            @pl.when((block >= base) & (block < base + 4))
            def _():
                to = pl.ds(pl.multiple_of((block - base) * BLK, BLK), BLK)
                ref[0, to, :] = tile[rows : rows + BLK]
                ref[1, to, :] = tile[2 * BLK + rows : 3 * BLK + rows]


def attend_kernel(after, meta, q_own, qkv_next, kv_mine, kv_theirs, gains, tables, *refs):
    q_ref, own_ref, oth_ref, ot_ref, inv_ref, w_ref, n_out, k_out, v_out = refs[10 + after : 19 + after]
    normed, normed_q, keys, values, values_t, acc, total, in_sem, n_sem, k_sem, v_sem = refs[19 + after :]
    for core in range(2):
        for p, (first, last, order) in enumerate(PARTS):
            size = last - first
            for half, steps in enumerate(held_by(order)):
                source, base = refs[half * 3 + p], 0
                if core == 1:
                    source = refs[6] if half == 0 else refs[7 + p]
                    base = 4 * first if half == 0 else 0
                for i, step in enumerate(steps):
                    row = first
                    while row < last:
                        block, inner = row // BLK, row % BLK
                        count = min(last - row, BLK - inner)
                        to = pl.multiple_of(meta[(core * 8 + step) * 4 + block] * BLK + inner, 16)
                        pltpu.make_async_copy(
                            source.at[pl.ds(base + i * size + row - first, count), :],
                            normed.at[pl.ds(to, count), :],
                            in_sem,
                        ).start()
                        row += count
    low = meta[66] == 0
    rows = w_ref.shape[0]
    first_core = jnp.where(low, kv_mine[:rows], kv_theirs[:rows])
    second_core = jnp.where(low, kv_theirs[:rows], kv_mine[:rows])
    quarter = HD // 4
    for kv in range(2):
        for side in range(2):
            at = side * 2 * quarter + kv * quarter
            to = kv * HD + side * 2 * quarter
            w_ref[:, to : to + 2 * quarter] = jnp.concatenate(
                [first_core[:, at : at + quarter], second_core[:, at : at + quarter]], axis=1
            )
    pltpu.make_async_copy(normed, normed, in_sem).wait()

    def prepare(chunk, carry):
        rows = rows_of(chunk)
        start = normed[rows, :].astype(F32)
        low_rows = (start * inverse_rms(start) * (1.0 + gains[0:1, :])).astype(BF16)
        normed[rows, :] = low_rows
        both = dot(low_rows, w_ref[...])
        cosine, sine = chunk_tables(tables, chunk)
        first, second = both[:, :HALF], both[:, HALF:HD]
        keys[rows, :HALF] = (first * cosine - second * sine).astype(BF16)
        keys[rows, HALF:] = (second * cosine + first * sine).astype(BF16)
        low = both[:, HD:].astype(BF16)
        values[rows, :] = low
        values_t[chunk] = low.T
        return carry

    lax.fori_loop(0, chunks_needed(meta), prepare, 0)
    copies = [
        pltpu.make_async_copy(normed, n_out, n_sem),
        pltpu.make_async_copy(keys, k_out, k_sem),
        pltpu.make_async_copy(values, v_out, v_sem),
    ]
    for copy in copies:
        copy.start()
    for b in range(8):
        normed_q[b * BLK : (b + 1) * BLK, :] = normed[block_rows(q_block(meta, b)), :]
    for h, weight in enumerate((q_own[...], qkv_next[: q_own.shape[0], :HD])):
        pre = dot(normed_q[...], weight) * HD ** (-0.5)
        for b in range(8):
            cosine, sine = block_tables(tables, q_block(meta, b))
            first = pre[b * BLK : (b + 1) * BLK, :HALF]
            second = pre[b * BLK : (b + 1) * BLK, HALF:]
            q_ref[h, b, :, :HALF] = (first * cosine - second * sine).astype(BF16)
            q_ref[h, b, :, HALF:] = (second * cosine + first * sine).astype(BF16)

    def tile(t, carry):
        b0, b1, chunks, limit = tile_facts(meta, t)
        queries = tile_rows(q_ref, b0, b1)
        acc[...] = jnp.zeros_like(acc)
        total[...] = jnp.zeros_like(total)

        def step(chunk, masked):
            scores = dot_nt(keys[rows_of(chunk), :], queries)
            grown = jnp.exp2(CAP_LOG2 * jnp.tanh(scores * (1.0 / CAP)))
            if masked:
                at = lax.broadcasted_iota(jnp.int32, (CHUNK, 4 * BLK), 0)
                grown = jnp.where(at <= limit - chunk * CHUNK, grown, 0.0)
            total[...] += jnp.sum(grown.reshape(CHUNK // 8, 8, 4 * BLK), axis=0)
            acc[...] += dot(values_t[chunk], grown.astype(BF16))

        over_chunks(step, whole_chunks(meta, t), chunks)
        whole = jnp.sum(total[...], axis=0, keepdims=True)
        inverse = jnp.where(whole > 0.0, 1.0 / jnp.where(whole > 0.0, whole, 1.0), 0.0)
        mixed = acc[...] * inverse
        shift = -jnp.log2(jnp.where(whole > 0.0, whole, 1.0))
        inv_ref[t] = jnp.broadcast_to(shift, (8, 4 * BLK))
        ot_ref[t] = mixed.astype(BF16)
        put_tile(own_ref, oth_ref, b0, b1, mixed.T.astype(BF16))
        return carry

    lax.fori_loop(0, 4, tile, 0)
    for copy in copies:
        copy.wait()


def attend_back_kernel(
    meta, q_ref, do_own, pack_oth, ot_ref, inv_ref, q_own, qkv_next, tables, k_in, v_in, feed_terms,
    dq_ref, both_ref, dn_own, dn_give, near_ref, far_ref, *refs
):
    do_ref, do_oth, k_ref, v_ref, keys_t, d_keys, d_values, d_both, acc, do_sem, k_sem, v_sem, both_sem, out_sem = refs
    loads = [
        pltpu.make_async_copy(k_in, k_ref, k_sem),
        pltpu.make_async_copy(v_in, v_ref, v_sem),
    ]
    for load in loads:
        load.start()
    first = pack_oth.shape[1] - 2 * HD
    do_copy = pltpu.make_async_copy(pack_oth.at[:, pl.ds(first, 2 * HD)], do_oth, do_sem)
    do_copy.start()
    do_copy.wait()
    for h in range(2):
        for b in range(4):
            rows = slice(b * BLK, (b + 1) * BLK)
            do_ref[h, b] = do_own[h, rows]
            do_ref[h, 4 + b] = do_oth[rows, h * HD : (h + 1) * HD]
    needed = chunks_needed(meta)
    loads[0].wait()

    def prepare(chunk, carry):
        rows = rows_of(chunk)
        keys_t[chunk] = k_ref[rows, :].T
        d_keys[rows, :] = jnp.zeros((CHUNK, HD), F32)
        d_values[rows, :] = jnp.zeros((CHUNK, HD), F32)
        return carry

    lax.fori_loop(0, needed, prepare, 0)
    loads[1].wait()

    def tile(t, carry):
        b0, b1, chunks, limit = tile_facts(meta, t)
        queries = tile_rows(q_ref, b0, b1)
        grads = tile_rows(do_ref, b0, b1)
        shift = inv_ref[t, 0:1, :]
        grads_t = grads.astype(F32).T
        center = jnp.sum(grads_t * ot_ref[t].astype(F32), axis=0, keepdims=True)
        acc[...] = jnp.zeros_like(acc)

        def step(chunk, masked):
            rows = rows_of(chunk)
            scores = dot_nt(k_ref[rows, :], queries)
            ratio = jnp.tanh(scores * (1.0 / CAP))
            probs = jnp.exp2(CAP_LOG2 * ratio + shift)
            if masked:
                at = lax.broadcasted_iota(jnp.int32, (CHUNK, 4 * BLK), 0)
                probs = jnp.where(at <= limit - chunk * CHUNK, probs, 0.0)
            d_probs = dot_nt(v_ref[rows, :], grads)
            d_scores = (probs * (d_probs - center) * (1.0 - ratio * ratio)).astype(BF16)
            d_values[rows, :] += dot(probs.astype(BF16), grads)
            d_keys[rows, :] += dot(d_scores, queries)
            acc[...] += dot(keys_t[chunk], d_scores)

        over_chunks(step, whole_chunks(meta, t), chunks)
        turned = acc[...].T * HD ** (-0.5)
        for i, (block, place) in enumerate(((b0, 80 + 2 * t), (b1, 81 + 2 * t))):
            cosine, sine = block_tables(tables, meta[place])
            for h in range(2):
                part = turned[(2 * h + i) * BLK : (2 * h + i + 1) * BLK]
                first, second = part[:, :HALF], part[:, HALF:]
                dq_ref[block_rows(block), h * HD : h * HD + HALF] = (
                    first * cosine + second * sine
                ).astype(BF16)
                dq_ref[block_rows(block), h * HD + HALF : (h + 1) * HD] = (
                    second * cosine - first * sine
                ).astype(BF16)
        return carry

    lax.fori_loop(0, 4, tile, 0)

    def finish(chunk, carry):
        rows = rows_of(chunk)
        cosine, sine = chunk_tables(tables, chunk)
        first, second = d_keys[rows, :HALF], d_keys[rows, HALF:]
        d_both[rows, :HALF] = (first * cosine + second * sine).astype(BF16)
        d_both[rows, HALF:HD] = (second * cosine - first * sine).astype(BF16)
        d_both[rows, HD:] = d_values[rows, :].astype(BF16)
        return carry

    lax.fori_loop(0, needed, finish, 0)

    def clear(chunk, carry):
        d_both[rows_of(chunk), :] = jnp.zeros((CHUNK, 2 * HD), BF16)
        return carry

    lax.fori_loop(needed, SLOTS // CHUNK, clear, 0)
    for n in range(16):
        for b in range(4):
            target = near_ref.at[n] if n < 8 else far_ref.at[n - 8]
            pltpu.make_async_copy(
                d_both.at[block_rows(meta[n * 4 + b]), :], target.at[pl.ds(b * BLK, BLK), :], out_sem
            ).start()

    whole = pltpu.make_async_copy(d_both, both_ref, both_sem)
    whole.start()
    q_next = qkv_next[: q_own.shape[0], :HD]
    partial = dot_nt(dq_ref[:, :HD], q_own[...]) + dot_nt(dq_ref[:, HD:], q_next)
    dn_own[...] = partial[: 4 * BLK]
    dn_give[...] = partial[4 * BLK :].astype(BF16)
    whole.wait()
    pltpu.make_async_copy(d_both, d_both, out_sem).wait()


def proj_grads_kernel(meta, dq, q_own, qkv_next, kv_w, gains, gain_in, both_in, n_in, terms_ref, give_ref, *refs):
    normed, both, normed_q, kv_grad, n_sem, b_sem = refs
    loads = [pltpu.make_async_copy(both_in, both, b_sem), pltpu.make_async_copy(n_in, normed, n_sem)]
    for load in loads:
        load.start()
    for load in loads:
        load.wait()
    kv_grad[...] = jnp.zeros_like(kv_grad)

    def add(chunk, carry):
        rows = rows_of(chunk)
        kv_grad[...] += dot_tn(both[rows, :], normed[rows, :])
        return carry

    lax.fori_loop(0, chunks_needed(meta), add, 0)
    for b in range(8):
        normed_q[b * BLK : (b + 1) * BLK, :] = normed[block_rows(q_block(meta, b)), :]
    q_next = qkv_next[: q_own.shape[0], :HD]
    weighed = jnp.sum(kv_grad[...] * kv_w[...].T.astype(F32), axis=0, keepdims=True)
    for h, weight in enumerate((q_own[...], q_next)):
        q_grad = dot_tn(dq[:, h * HD : (h + 1) * HD], normed_q[...])
        weighed = weighed + jnp.sum(q_grad * weight.T.astype(F32), axis=0, keepdims=True)
        terms_ref[h, :HD, :] = q_grad
    gain_rows = jnp.concatenate(
        [weighed / (1.0 + gains[0:1, :]), gain_in[1:8, :], jnp.zeros((8, gains.shape[1]), F32)], axis=0
    )
    yh, c = meta[65], meta[66]
    quarter = HD // 4
    for h in range(2):
        side = yh if h == 0 else 1 - yh
        for kv in range(2):
            mine = pl.ds(pl.multiple_of(kv * HD + (2 * side + c) * quarter, quarter), quarter)
            theirs = pl.ds(pl.multiple_of(kv * HD + (2 * side + 1 - c) * quarter, quarter), quarter)
            terms_ref[h, HD + kv * quarter : HD + (kv + 1) * quarter, :] = kv_grad[mine, :]
            at = h * 2 * quarter + kv * quarter
            give_ref[at : at + quarter, :] = kv_grad[theirs, :].astype(BF16)
        terms_ref[h, HD + 2 * quarter : HD + 2 * quarter + 16, :] = gain_rows
        terms_ref[h, HD + 2 * quarter + 16 :, :] = jnp.zeros((2 * quarter - 16, gains.shape[1]), F32)
    give_ref[4 * quarter :, :] = gain_rows.astype(BF16)


def attend(meta, weights, gains, tables, pieces, after):
    width = pieces[0].shape[1]
    return pl.pallas_call(
        functools.partial(attend_kernel, len(after)),
        out_shape=(
            shape((2, 8, BLK, HD), BF16),
            shape((2, 4 * BLK, HD), BF16),
            shape((2, 4 * BLK, HD), BF16),
            shape((4, HD, 4 * BLK), BF16),
            shape((4, 8, 4 * BLK), F32),
            shape((width, 2 * HD), BF16),
            shape((SLOTS, width), BF16),
            shape((SLOTS, HD), BF16),
            shape((SLOTS, HD), BF16),
        ),
        in_specs=[SMEM_SPEC] + [VMEM_SPEC] * 6 + [ANY_SPEC] * (10 + len(after)),
        out_specs=(VMEM_SPEC,) * 6 + (HBM_SPEC,) * 3,
        scratch_shapes=[
            pltpu.VMEM((SLOTS, width), BF16),
            pltpu.VMEM((8 * BLK, width), BF16),
            pltpu.VMEM((SLOTS, HD), BF16),
            pltpu.VMEM((SLOTS, HD), BF16),
            pltpu.VMEM((SLOTS // CHUNK, HD, CHUNK), BF16),
            pltpu.VMEM((HD, 4 * BLK), F32),
            pltpu.VMEM((8, 4 * BLK), F32),
            DMA,
            DMA,
            DMA,
            DMA,
        ],
        compiler_params=params(VMEM),
        cost_estimate=cost(20, 20),
        name="attend",
    )(meta, *weights, gains, tables, *pieces, *after)


def attend_back(meta, queries, d_own, pack_oth, mixed_t, inverse, weights, tables, keys, values, after):
    width = weights[0].shape[0]
    rows = 4 * BLK
    return pl.pallas_call(
        attend_back_kernel,
        out_shape=(
            shape((2 * rows, 2 * HD), BF16),
            shape((SLOTS, 2 * HD), BF16),
            shape((rows, width), F32),
            shape((rows, width), BF16),
            shape((8, rows, 2 * HD), BF16),
            shape((8, rows, 2 * HD), BF16),
        ),
        in_specs=[SMEM_SPEC] + [VMEM_SPEC] * 2 + [ANY_SPEC] + [VMEM_SPEC] * 5 + [HBM_SPEC] * 2 + [ANY_SPEC],
        out_specs=(VMEM_SPEC, HBM_SPEC, VMEM_SPEC, VMEM_SPEC, ANY_SPEC, ANY_SPEC),
        scratch_shapes=[
            pltpu.VMEM((2, 8, BLK, HD), BF16),
            pltpu.VMEM((rows, 2 * HD), BF16),
            pltpu.VMEM((SLOTS, HD), BF16),
            pltpu.VMEM((SLOTS, HD), BF16),
            pltpu.VMEM((SLOTS // CHUNK, HD, CHUNK), BF16),
            pltpu.VMEM((SLOTS, HD), F32),
            pltpu.VMEM((SLOTS, HD), F32),
            pltpu.VMEM((SLOTS, 2 * HD), BF16),
            pltpu.VMEM((HD, 4 * BLK), F32),
            DMA,
            DMA,
            DMA,
            DMA,
            DMA,
        ],
        compiler_params=params(VMEM),
        cost_estimate=cost(40, 30),
        name="attend_back",
    )(meta, queries, d_own, pack_oth, mixed_t, inverse, *weights, tables, keys, values, *after)


def proj_grads(meta, dq, weights, gains, gain_in, both, normed):
    width = normed.shape[1]
    return pl.pallas_call(
        proj_grads_kernel,
        out_shape=(shape((2, 2 * HD, width), F32), shape((HD + 16, width), BF16)),
        in_specs=[SMEM_SPEC] + [VMEM_SPEC] * 6 + [HBM_SPEC] * 2,
        out_specs=(VMEM_SPEC,) * 2,
        scratch_shapes=[
            pltpu.VMEM((SLOTS, width), BF16),
            pltpu.VMEM((SLOTS, 2 * HD), BF16),
            pltpu.VMEM((8 * BLK, width), BF16),
            pltpu.VMEM((2 * HD, width), F32),
            DMA,
            DMA,
        ],
        compiler_params=params(VMEM),
        cost_estimate=cost(2, 12),
        name="proj_grads",
    )(meta, dq, *weights, gains, gain_in, both, normed)


GELU_A, GELU_B = 0.7978845608028654, 0.044715


def feed_kernel(meta, gains, mix_own, mix_oth, tok0, tok1, cot0, cot1, *refs):
    weights = refs[:8]
    result0, result1, d_middle_ref, keep_mix, pack, keep, gain_ref = refs[8:15]
    wdo, wgu, zs, sems = refs[15:]
    rows, width = 2 * tok0.shape[0], tok0.shape[1]
    hid = wgu.shape[2] // 2
    copies = [pltpu.make_async_copy(weights[s], wdo.at[s], sems.at[s]) for s in range(4)]
    copies += [pltpu.make_async_copy(weights[4 + s], wgu.at[s], sems.at[4 + s]) for s in range(4)]
    for copy in copies:
        copy.start()
    gain_b, gain_c, gain_d = gains[1:2, :], gains[2:3, :], gains[3:4, :]
    valid = []
    for b in range(4):
        inner = lax.broadcasted_iota(jnp.int32, (BLK, 1), 0)
        valid.append(meta[b] * BLK + inner < meta[64])
    valid = jnp.concatenate([v.astype(F32) for v in valid], axis=0) > 0.5
    start = jnp.concatenate([tok0[...].astype(F32), tok1[...].astype(F32)], axis=0)
    branch = jnp.zeros((rows, width), F32)
    for s in range(4):
        copies[s].wait()
        mixed = mix_own[s] if s < 2 else mix_oth[s - 2]
        branch = branch + dot(mixed, wdo[s, hid:, :])
    middle = start + branch * inverse_rms(branch) * (1.0 + gain_b)
    second = (middle * inverse_rms(middle) * (1.0 + gain_c)).astype(BF16)
    pack[:, :width] = second
    output = jnp.zeros((rows, width), F32)
    at = 3 * width
    for s in range(4):
        copies[4 + s].wait()
        both = dot(second, wgu[s])
        zs[s] = both
        gate, up = both[:, :hid], both[:, hid:]
        bent = jnp.tanh(GELU_A * (gate + GELU_B * gate * gate * gate))
        hidden = (0.5 * gate * (1.0 + bent) * up).astype(BF16)
        if s < 2:
            keep[:, s * hid : (s + 1) * hid] = hidden
        else:
            pack[:, at + (s - 2) * hid : at + (s - 1) * hid] = hidden
        output = output + dot(hidden, wdo[s, :hid, :])
    result = jnp.where(
        valid, middle + output * inverse_rms(output) * (1.0 + gain_d), 0.0
    ).astype(BF16)
    result0[...] = result[: rows // 2]
    result1[...] = result[rows // 2 :]
    cot = jnp.concatenate([cot0[...].astype(F32), cot1[...].astype(F32)], axis=0)
    seed = jnp.where(valid, cot, 0.0)
    d_output, d_gain_d = norm_back(output, gain_d, seed)
    d_output = d_output.astype(BF16)
    pack[:, width : 2 * width] = d_output
    d_second = jnp.zeros((rows, width), F32)
    for s in range(4):
        d_hidden = dot_nt(d_output, wdo[s, :hid, :])
        gate, up = zs[s, :, :hid], zs[s, :, hid:]
        square = gate * gate
        bent = jnp.tanh(GELU_A * gate * (1.0 + GELU_B * square))
        slope = 0.5 * (1.0 + bent) + (0.5 * GELU_A) * gate * (1.0 - bent * bent) * (
            1.0 + 3.0 * GELU_B * square
        )
        d_gate = (d_hidden * up * slope).astype(BF16)
        d_up = (d_hidden * (0.5 * gate * (1.0 + bent))).astype(BF16)
        if s < 2:
            where = 2 * hid + s * 2 * hid
            keep[:, where : where + hid] = d_gate
            keep[:, where + hid : where + 2 * hid] = d_up
        else:
            where = at + 2 * hid + (s - 2) * 2 * hid
            pack[:, where : where + hid] = d_gate
            pack[:, where + hid : where + 2 * hid] = d_up
        d_second = d_second + dot_nt(d_gate, wgu[s, :, :hid]) + dot_nt(d_up, wgu[s, :, hid:])
    d_mid, d_gain_c = norm_back(middle, gain_c, d_second)
    d_middle = seed + d_mid
    d_middle_ref[...] = d_middle
    d_branch, d_gain_b = norm_back(branch, gain_b, d_middle)
    d_branch = d_branch.astype(BF16)
    pack[:, 2 * width : 3 * width] = d_branch
    for s in range(4):
        d_mixed = dot_nt(d_branch, wdo[s, hid:, :]).astype(BF16)
        if s < 2:
            keep_mix[s] = d_mixed
        else:
            pack[:, at + 6 * hid + (s - 2) * HD : at + 6 * hid + (s - 1) * HD] = d_mixed
    zero = jnp.zeros((1, width), F32)
    gain_ref[...] = jnp.concatenate(
        [zero, d_gain_b[None], d_gain_c[None], d_gain_d[None], zero, zero, zero, zero], axis=0
    )


def feed(meta, gains, mix_own, mix_oth, tok, cot, do_weights, gu_weights):
    rows, width = 2 * tok[0].shape[0], tok[0].shape[1]
    hid = gu_weights[0].shape[1] // 2
    do_rows = do_weights[0].shape[0]
    return pl.pallas_call(
        feed_kernel,
        out_shape=(
            shape((rows // 2, width), BF16),
            shape((rows // 2, width), BF16),
            shape((rows, width), F32),
            shape((2, rows, HD), BF16),
            shape((rows, 3 * width + 6 * hid + 2 * HD), BF16),
            shape((rows, 6 * hid), BF16),
            shape((8, width), F32),
        ),
        in_specs=[SMEM_SPEC] + [VMEM_SPEC] * 7 + [ANY_SPEC] * 8,
        out_specs=(VMEM_SPEC,) * 7,
        scratch_shapes=[
            pltpu.VMEM((4, do_rows, width), BF16),
            pltpu.VMEM((4, width, 2 * hid), BF16),
            pltpu.VMEM((4, rows, 2 * hid), F32),
            pltpu.SemaphoreType.DMA((8,)),
        ],
        compiler_params=params(VMEM),
        cost_estimate=cost(5, 16),
        name="feed",
    )(meta, gains, mix_own, mix_oth, *tok, *cot, *do_weights, *gu_weights)


QKV = 32


def feed_grads_kernel(own, oth, keep, mix_own, mix_oth, out_ref):
    hid = keep.shape[1] // 6
    share, width = out_ref.shape[3:]
    at = 3 * width

    def put(s, first, value):
        row, last = first, first + value.shape[0]
        while row < last:
            to, inner = row // share, row % share
            count = min(last - row, share - inner)
            part = value[row - first : row - first + count]
            out_ref[to % 4, to // 4, s, inner : inner + count, :] = part
            row += count

    for s in range(2):
        for part in range(2):
            mine = 2 * hid + (2 * s + part) * hid
            theirs = at + 2 * hid + (2 * s + part) * hid
            value = dot_tn(keep[:, mine : mine + hid], own[:, :width])
            value = value + dot_tn(oth[:, theirs : theirs + hid], oth[:, :width])
            put(s, part * hid, value.astype(BF16))
        value = dot_tn(keep[:, s * hid : (s + 1) * hid], own[:, width : 2 * width])
        value = value + dot_tn(oth[:, at + s * hid : at + (s + 1) * hid], oth[:, width : 2 * width])
        put(s, 2 * hid, value.astype(BF16))
        value = dot_tn(mix_own[s], own[:, 2 * width : 3 * width])
        value = value + dot_tn(mix_oth[s], oth[:, 2 * width : 3 * width])
        put(s, 3 * hid, value.astype(BF16))


def share_sum_kernel(got, *outs):
    for s, out in enumerate(outs):
        total = got[0, s].astype(F32)
        for n in range(1, 16):
            total = total + got[n, s].astype(F32)
        out[...] = total.astype(BF16)


def total_kernel(a, b, c, d, out):
    total = a[...].astype(F32) + b[...].astype(F32) + c[...].astype(F32) + d[...].astype(F32)
    out[...] = total.astype(BF16)


def total_wide_kernel(a, b, c, d, out):
    total = a[...].astype(F32) + b[...].astype(F32) + c[...].astype(F32) + d[...].astype(F32)
    out[...] = jnp.broadcast_to(total.astype(BF16)[None], out.shape)


def feed_out_kernel(got, gate, up, down, out):
    hid = gate.shape[1]
    whole = jnp.concatenate([got[n].astype(F32) for n in range(16)], axis=0)
    gate[...] = whole[:hid].T
    up[...] = whole[hid : 2 * hid].T
    down[...] = whole[2 * hid : 3 * hid]
    out[...] = whole[3 * hid :]


def qkv_out_kernel(got, q_out, k_out, v_out, gain_out):
    small = jnp.concatenate([got[n].astype(F32) for n in range(16)], axis=0)
    quarter = HD // 4
    q_out[...] = small[:HD].T
    k_out[...] = small[HD : HD + quarter]
    v_out[...] = small[HD + quarter : HD + 2 * quarter]
    gain_out[...] = small[HD + 2 * quarter : HD + 2 * quarter + 8]


def sum_a_kernel(near, far, g0, g1, k0, k1):
    gives, keeps = (g0, g1), (k0, k1)
    for p, (first, last, (a, b, d)) in enumerate(BACK_PARTS):
        size = last - first
        for i, move in enumerate((0, a, b, a | b)):
            rows = pl.ds(i * size, size)
            for out, at in ((keeps[p], move), (gives[p], move | d)):
                both = near[at, first:last].astype(F32) + far[at, first:last].astype(F32)
                out[rows, :] = both.astype(out.dtype)


def qkv_shares_kernel(terms, got, shares):
    half = HD // 2
    for h in range(2):
        for n in range(16):
            at = n * QKV
            value = terms[h, at : at + QKV]
            if HD <= at < HD + half:
                from_row = h * half + at - HD
                value = value + got[from_row : from_row + QKV].astype(F32)
            if at == HD + half:
                rest = jnp.zeros((QKV - 16, terms.shape[2]), F32)
                value = value + jnp.concatenate([got[HD:].astype(F32), rest], axis=0)
            shares[n, h] = value.astype(BF16)


def halves(keeps, gots, outs):
    for p in range(2):
        rows = keeps[p].shape[0] // 2
        outs[p][...] = (keeps[p][rows:] + gots[p][rows:].astype(F32)).astype(BF16)
        outs[2 + p][...] = keeps[p][:rows] + gots[p][:rows].astype(F32)


def sum_b_kernel(k0, k1, g0, g1, *outs):
    halves((k0, k1), (g0, g1), outs)


def sum_d_kernel(k0, k1, g0, g1, dn, dn_got, tok0, tok1, d_middle, kv_w, gains, t0, t1):
    d_kv = [k[...] + g[...].astype(F32) for k, g in ((k0, g0), (k1, g1))]
    d_kv = jnp.concatenate(d_kv, axis=0).astype(BF16)
    d_normed = dn[...] + dn_got[...].astype(F32) + dot_nt(d_kv, kv_w[...])
    start = jnp.concatenate([tok0[...].astype(F32), tok1[...].astype(F32)], axis=0)
    d_start, _ = norm_back(start, gains[0:1, :], d_normed)
    grads = (d_middle[...] + d_start).astype(BF16)
    half = t0.shape[0]
    t0[...] = grads[:half]
    t1[...] = grads[half:]


def on_device(
    tokens,
    cotangent,
    lengths,
    block_order,
    query_weight,
    key_weight,
    value_weight,
    out_weight,
    gate_weight,
    up_weight,
    down_weight,
    gain_attn_in,
    gain_attn_out,
    gain_ffn_in,
    gain_ffn_out,
):
    ctx, fsdp = lax.axis_index("ctx"), lax.axis_index("fsdp")
    yl, z, x = ctx // 16, (ctx // 4) % 4, ctx % 4
    yh, c = fsdp // 2, fsdp % 2
    zh, zl, xh, xl = z // 2, z % 2, x // 2, x % 2
    low_y, low_c, low_x = yh == 0, c == 0, xh == 0
    own_rows = 4 * BLK
    width = tokens.shape[-1]

    def rows_to(array):
        return (
            send(jnp.where(low_x, array[0, 0], array[0, 1]), regroup(0)),
            send(jnp.where(low_x, array[0, 1], array[0, 0]), regroup(1)),
        )

    def rows_back(first, second):
        first, second = send(first, regroup(0)), send(second, regroup(1))
        return jnp.stack([jnp.where(low_x, first, second), jnp.where(low_x, second, first)])[None]

    tok0, tok1 = rows_to(tokens)
    part_shapes = [shape((size, width), BF16) for size in sizes()]
    spot = jnp.stack([yh, c, zh, zl, xh, xl, yl, fsdp]).astype(jnp.int32)
    part_shapes = [shape((size, width), BF16) for size in sizes()]
    heads = HD
    quarter = key_weight.shape[1]
    hidden_cols = gate_weight.shape[1]
    share = gain_attn_in.shape[0]
    length_parts = jnp.concatenate([lengths // 64, lengths % 64], axis=0).astype(BF16)
    gains = jnp.stack([gain_attn_in, gain_attn_out, gain_ffn_in, gain_ffn_out])
    gains = jnp.concatenate([gains, jnp.pad(length_parts, ((0, 0), (0, share - 2)))], axis=0)
    (qkv_own,) = step(
        pack_qkv_kernel,
        [shape((width + 16, heads + 2 * quarter), BF16)],
        (query_weight, key_weight.T, value_weight.T, gains),
        mbytes=6,
        name="pack_qkv",
    )
    qkv_next = send(qkv_own, to_next)
    parts = step(cut_kernel, part_shapes, (tok0, tok1), after=(qkv_own,), mbytes=6, name="cut")

    def cube_send(arrays, stage):
        return [send(array, to_cube(order[stage])) for array, (first, last, order) in zip(arrays, PARTS)]

    got = cube_send(parts, 0)

    (do_own,) = step(
        pack_rows_kernel,
        [shape((hidden_cols + heads, width), BF16)],
        (down_weight, out_weight),
        after=(parts[0],),
        name="pack_do",
    )
    do_next = send(do_own, to_next)
    pairs = step(
        functools.partial(join_kernel, 3),
        [shape((2 * size, width), BF16) for size in sizes()],
        (*parts, *got),
        after=(do_own,),
        mbytes=6,
        name="join",
    )
    got = cube_send(pairs, 1)

    (kv_pair,) = step(
        kv_pair_kernel,
        [shape((width + 32, 4 * quarter), BF16)],
        (qkv_own, qkv_next),
        meta=spot,
        mbytes=6,
        name="kv_pair",
    )
    kv_other = send(kv_pair, to_core)
    mine, theirs = (
        m[width:, :share].reshape(2, 16, share)[:, :6] for m in (kv_pair, kv_other)
    )
    quarters = jnp.stack(
        [jnp.where(low_c, mine, theirs), jnp.where(low_c, theirs, mine)], axis=1
    )
    all_gains = jnp.transpose(quarters[:, :, :4], (2, 0, 1, 3)).reshape(4, width).astype(F32)
    gain_rows = jnp.concatenate([all_gains, jnp.zeros((4, width), F32)], axis=0)
    lengths_here = jnp.where(low_y, quarters[0, :, 4:, :2], quarters[1, :, 4:, :2])
    lengths_here = jnp.where(zh == 0, lengths_here[0], lengths_here[1]).astype(jnp.int32)
    lengths_here = lengths_here[0] * 64 + lengths_here[1]
    length = jnp.where(low_x, lengths_here[0], lengths_here[1])

    joined = step(
        join_all_kernel,
        [shape((4 * size, width), BF16) for size in sizes()] + [shape((4 * own_rows, width), BF16)],
        (*pairs, *got),
        after=(kv_pair,),
        mbytes=8,
        name="join_all",
    )
    low_parts, low_all = joined[:3], joined[3]
    high_parts = cube_send(low_parts, 2)
    (gu_own,) = step(
        pack_columns_kernel,
        [shape((width, 2 * hidden_cols), BF16)],
        (gate_weight, up_weight),
        after=(do_next, joined[0]),
        name="pack_gu",
    )

    stored = []
    for other in range(2):
        for move in range(8):
            dy, dz, dx = move >> 2, (move >> 1) & 1, move & 1
            for turn in range(2):
                place = (yl ^ dy) * 16 + ((c ^ other) * 2 + (zl ^ dz)) * 4
                place = place + (xh ^ turn) * 2 + (xl ^ dx)
                stored += [place * 2, place * 2 + 1]
    stored = jnp.stack(stored)
    slots = jnp.arange(64, dtype=jnp.int32)
    block_at = jnp.sum(
        jnp.where(stored[:, None] == slots[None, :], block_order[None, :], 0), axis=1
    ).astype(jnp.int32)
    q_blocks = jnp.concatenate([block_at[0:4], block_at[32:36]])
    rank = jnp.sum((q_blocks[None, :] < q_blocks[:, None]).astype(jnp.int32), axis=1)
    eight = jnp.arange(8, dtype=jnp.int32)
    chosen = rank[None, :] == eight[:, None]
    order = jnp.sum(jnp.where(chosen, eight[None, :], 0), axis=1).astype(jnp.int32)
    order_block = jnp.sum(jnp.where(chosen, q_blocks[None, :], 0), axis=1).astype(jnp.int32)
    facts = jnp.stack([length, yh, c, zh, xh, x, z, z]).astype(jnp.int32)
    meta = jnp.concatenate([block_at, facts, order, order_block])

    low_all = send(low_all, to_core)
    high_far = [send(part, to_core) for part in high_parts]
    pieces = list(low_parts) + high_parts + [low_all] + high_far
    tables = jnp.asarray(angle_tables())
    gu_next = send(gu_own, to_next)
    (do_late,) = gate((do_own,), (high_parts[2],))
    do_swap, do_next_swap = send(do_late, to_core), send(do_next, to_core)
    do_weights = [do_late, do_next, do_swap, do_next_swap]
    gu_swap = send(gu_own, to_core)
    half_shape = shape((own_rows // 2, width), BF16)
    cot0, cot1 = step(
        pick_kernel,
        [half_shape, half_shape],
        (cotangent[0],),
        after=(joined[0],),
        meta=spot,
        mbytes=6,
        name="pick_cot",
    )
    cot0, cot1 = send(cot0, regroup(0)), send(cot1, regroup(1))
    queries, mix_own, mix_oth, mixed_t, inverse, kv_weight, sorted_normed, keys, values = attend(
        meta, (query_weight, qkv_next, kv_pair, kv_other), gain_rows, tables, pieces, (do_swap, do_next_swap, gu_swap)
    )

    (gu_next,) = gate((gu_next,), (mix_own, cot0, cot1))
    gu_weights = [gu_own, gu_next, gu_swap, send(gu_next, to_core)]
    result0, result1, d_middle, keep_mix, pack, keep, gain_terms = feed(
        meta, gain_rows, mix_own, send(mix_oth, to_core), (tok0, tok1), (cot0, cot1), do_weights, gu_weights
    )
    pack_oth = send(pack, to_core)
    span = 3 * hidden_cols + HD
    (feed_shares,) = step(
        feed_grads_kernel,
        [shape((4, 4, 2, span // 16, width), BF16)],
        (pack, pack_oth, keep, mix_own, mix_oth),
        name="feed_grads",
    )
    feed_sums = lax.psum_scatter(feed_shares, "ctx", scatter_dimension=0, axis_index_groups=ROWS)

    dq, d_both, dn_own, dn_give, d_near, d_far = attend_back(
        meta,
        queries,
        keep_mix,
        pack_oth,
        mixed_t,
        inverse,
        (query_weight, qkv_next),
        tables,
        keys,
        values,
        (feed_shares,),
    )
    d_far, dn_got = send(d_far, to_core), send(dn_give, to_core)

    def part_shape(count, dtype):
        return [shape((count * (last - first), 2 * HD), dtype) for first, last, order in BACK_PARTS]

    def rows_shape(*dims):
        return shape((*dims, width), BF16)

    def cube_return(arrays, stage):
        return [
            send(array, to_cube(order[stage])) for array, (first, last, order) in zip(arrays, BACK_PARTS)
        ]

    def over_y(mine, theirs):
        return mine, send(mine, to_yl), send(theirs, to_next), send(theirs, to_yh)

    outs = step(
        sum_a_kernel, part_shape(4, BF16) + part_shape(4, F32), (d_near, d_far), name="sum_a"
    )
    got, keeps = cube_return(outs[:2], 2), outs[2:4]
    terms, core_give = proj_grads(
        meta, dq, (query_weight, qkv_next, kv_weight), gain_rows, gain_terms, d_both, sorted_normed
    )
    core_got = send(core_give, to_core)
    (qkv_shares,) = step(
        qkv_shares_kernel, [rows_shape(16, 2, QKV)], (terms, core_got), name="qkv_shares"
    )
    (feed_sums,) = gate((feed_sums,), (qkv_shares,))
    feed_sums = lax.psum_scatter(feed_sums, "ctx", scatter_dimension=0, axis_index_groups=COLUMNS)
    outs = step(
        sum_b_kernel,
        part_shape(2, BF16) + part_shape(2, F32),
        (*keeps, *got),
        after=(qkv_shares,),
        name="sum_b",
    )
    got, keeps = cube_return(outs[:2], 1), outs[2:4]
    (feed_sums,) = gate((feed_sums,), (outs[0],))
    feed_terms = over_y(feed_sums[0], feed_sums[1])
    (feed_all,) = step(
        total_kernel, [rows_shape(span // 16)], feed_terms, after=(*got,), name="feed_total"
    )
    outs = step(
        sum_b_kernel,
        part_shape(1, BF16) + part_shape(1, F32),
        (*keeps, *got),
        after=(feed_all,),
        name="sum_c",
    )
    got, keeps = cube_return(outs[:2], 0), outs[2:4]
    (qkv_shares,) = gate((qkv_shares,), (feed_terms[1],))
    qkv_got = swap_plane(qkv_shares)
    feed_all = lax.all_gather(feed_all, "ctx", axis_index_groups=PLANE)
    mine, theirs = step(
        share_sum_kernel, [rows_shape(QKV)] * 2, (qkv_got,), after=(qkv_shares,), name="qkv_sum"
    )
    qkv_terms = over_y(mine, theirs)
    (qkv_all,) = step(
        total_wide_kernel, [rows_shape(16, QKV)], qkv_terms, name="qkv_total"
    )
    tok_back0, tok_back1 = step(
        sum_d_kernel,
        [rows_shape(own_rows // 2)] * 2,
        (*keeps, *got, dn_own, dn_got, tok0, tok1, d_middle, kv_weight, gain_rows),
        after=(qkv_all,),
        name="sum_d",
    )
    token_block = rows_back(tok_back0, tok_back1).astype(F32)
    result0, result1 = gate((result0, result1), (qkv_terms[1],))
    result_block = rows_back(result0, result1)
    qkv_all = swap_plane(qkv_all)
    gate_grad, up_grad, down_grad, out_grad = step(
        feed_out_kernel,
        [
            shape((width, hidden_cols), F32),
            shape((width, hidden_cols), F32),
            shape((hidden_cols, width), F32),
            shape((HD, width), F32),
        ],
        (feed_all,),
        name="feed_out",
    )
    q_grad, k_grad, v_grad, gain_sum = step(
        qkv_out_kernel,
        [
            shape((width, HD), F32),
            shape((quarter, width), F32),
            shape((quarter, width), F32),
            shape((8, width), F32),
        ],
        (qkv_all,),
        after=(down_grad,),
        name="qkv_out",
    )
    share_rows = width // 4
    gain_grads = lax.dynamic_slice_in_dim(gain_sum, fsdp * share_rows, share_rows, axis=1)
    return (
        result_block,
        token_block,
        q_grad,
        k_grad.T,
        v_grad.T,
        out_grad,
        gate_grad,
        up_grad,
        down_grad,
        gain_grads[0],
        gain_grads[1],
        gain_grads[2],
        gain_grads[3],
    )


def solution(mesh):
    rows, cols, first = P("fsdp", None, "ctx", None), P(None, "fsdp"), P("fsdp", None)
    weights = (cols, cols, cols, first, cols, cols, first)
    gains = (P("fsdp"),) * 4
    return jax.shard_map(
        on_device,
        mesh=mesh,
        in_specs=(rows, rows, first, P()) + weights + gains,
        out_specs=(rows, rows) + weights + gains,
        check_vma=False,
    )
```
